512 devices in a mesh: row: 64 (over y, z), col: 8 (over x, core).
Axes of the slice: x: 4, y: 4, z: 16, core: 2. Of those that a mesh axis runs over, the one named last changes fastest.
Arguments:
- tiles: float32 [2048, 512, 512], P(('row', 'col'))
- tile_list: int32 [2048, 2], P(('row', 'col')), may hold values from 0 to 255, as said below
- tile_count: int32 [512], P(('row', 'col')), may hold values from 2 to 4, as said below
Outputs:
- row_scale: float32 [65536], P('row')
- col_scale: float32 [131072], P('col')
The draws below stay inside these ranges and needn't reach their ends.
Inputs may be any that keep to these rules, and one draw needn't show every extreme that they name: `tile_list`: each slot's tile lies in its device's block: tile-rows i * 2 to i * 2 + 1 and tile-columns j * 32 to j * 32 + 31 for device (i, j). The slots of one device name distinct tiles. Every tile-row and every tile-column of the matrix has a live tile. `tile_count`: some device has all 4 slots live.
All inputs are finite; a program needn't handle non-finite values.
Results may differ from the reference program's by a relative error of at most 0.0001.
Values sent between devices are 32-bit elements; how exact they have to be, the bound alone decides.
A program may use at most 64 MiB of HBM per device.

```python
import jax
import jax.numpy as jnp
from jax import lax

TILE = 512
TR_DEV = 2
TC_DEV = 32
SLOTS = 4
ROUNDS = 3
ROWS = 65536
COLS = 131072
TILES = 2048
N_ROW = 64
N_COL = 8


def draw_tiles(key, part):
    key = jax.random.fold_in(key, 11)
    first, second, third = jax.random.split(key, 3)
    base = jax.random.normal(first, (TILES, TILE, TILE), jnp.float32)
    spread = 10.0
    row_factor = jnp.exp(jax.random.uniform(second, (TILES, TILE, 1), jnp.float32) * jnp.log(spread))
    col_factor = jnp.exp(jax.random.uniform(third, (TILES, 1, TILE), jnp.float32) * jnp.log(spread))
    return base * row_factor * col_factor


def draw_tile_list(key, part):
    key = jax.random.fold_in(key, 23)
    devices = TILES // SLOTS
    col_devs = COLS // (TC_DEV * TILE)
    index = jnp.arange(devices, dtype=jnp.int32)
    row_dev = index // col_devs
    col_dev = index % col_devs
    first = 2 * col_dev % TR_DEV * TC_DEV + 2 * row_dev % TC_DEV
    second = (2 * col_dev + 1) % TR_DEV * TC_DEV + (2 * row_dev + 1) % TC_DEV
    keys = jax.random.split(key, devices)

    def picked(one_key, avoid_a, avoid_b):
        perm = jax.random.permutation(one_key, TR_DEV * TC_DEV)[:SLOTS].astype(jnp.int32)
        spots = jnp.arange(SLOTS, dtype=jnp.int32)
        taken = (perm == avoid_a) | (perm == avoid_b)
        order = jnp.argsort(jnp.where(taken, SLOTS + spots, spots))
        return perm[order[:SLOTS - 2]]
    extra = jax.vmap(picked)(keys, first, second)
    places = jnp.concatenate([first[:, None], second[:, None], extra], axis=1)
    tile_row = row_dev[:, None] * TR_DEV + places // TC_DEV
    tile_col = col_dev[:, None] * TC_DEV + places % TC_DEV
    return jnp.stack([tile_row, tile_col], axis=-1).reshape(TILES, 2).astype(jnp.int32)


def draw_tile_count(key, part):
    key = jax.random.fold_in(key, 37)
    devices = TILES // SLOTS
    first, second = jax.random.split(key)
    draws = jax.random.randint(first, (devices,), 0, 8)
    counts = jnp.where(draws < 5, 2, jnp.where(draws < 7, 3, SLOTS)).astype(jnp.int32)
    fullest = jax.random.randint(second, (), 0, devices)
    return counts.at[fullest].set(SLOTS).astype(jnp.int32)


def setup_inputs(seed: int = 0) -> dict:
    streams_of = jax.random.split(jax.random.key(seed), 4)
    tiles = draw_tiles(jax.random.fold_in(streams_of[3], 71), 0)
    tile_list = draw_tile_list(jax.random.fold_in(streams_of[3], 71), 0)
    tile_count = draw_tile_count(jax.random.fold_in(streams_of[3], 71), 0)
    return {"tiles": tiles, "tile_list": tile_list, "tile_count": tile_count}


EPS = 1e-06

def magnitudes(block, places, alive, row_scale, col_scale):
    left = row_scale[places[:, 0]]
    right = col_scale[places[:, 1]]
    return jnp.abs(left[:, :, None] * block * right[:, None, :]) * alive[:, None, None]

def reference(tiles, tile_list, tile_count):
    devices = N_ROW * N_COL
    blocks = tiles.reshape(devices, SLOTS, TILE, TILE)
    places = tile_list.reshape(devices, SLOTS, 2)
    alive = (jnp.arange(SLOTS, dtype=jnp.int32)[None, :] < tile_count[:, None]).astype(jnp.float32)
    row_index = tile_list[:, 0]
    col_index = tile_list[:, 1]

    def stats(row_scale, col_scale, use_max):

        def single(items):
            block, place, live = items
            magnitude = magnitudes(block, place, live, row_scale, col_scale)
            if use_max:
                return (lax.optimization_barrier(jnp.max(magnitude, axis=2)), lax.optimization_barrier(jnp.max(magnitude, axis=1)))
            return (lax.optimization_barrier(jnp.sum(magnitude, axis=2)), lax.optimization_barrier(jnp.sum(magnitude, axis=1)))
        row_part, col_part = lax.map(single, (blocks, places, alive))
        row_part = row_part.reshape(-1, TILE)
        col_part = col_part.reshape(-1, TILE)
        row_zero = jnp.zeros((ROWS // TILE, TILE), jnp.float32)
        col_zero = jnp.zeros((COLS // TILE, TILE), jnp.float32)
        if use_max:
            return (row_zero.at[row_index].max(row_part), col_zero.at[col_index].max(col_part))
        return (row_zero.at[row_index].add(row_part), col_zero.at[col_index].add(col_part))
    row_scale = jnp.ones((ROWS // TILE, TILE), jnp.float32)
    col_scale = jnp.ones((COLS // TILE, TILE), jnp.float32)
    for step in range(ROUNDS):
        row_peak, col_peak = stats(row_scale, col_scale, True)
        row_scale = row_scale / jnp.sqrt(row_peak + EPS)
        col_scale = col_scale / jnp.sqrt(col_peak + EPS)
    row_total, col_total = stats(row_scale, col_scale, False)
    row_scale = row_scale / jnp.sqrt(row_total + EPS)
    col_scale = col_scale / jnp.sqrt(col_total + EPS)
    return (row_scale.reshape(-1), col_scale.reshape(-1))
```

```python
import functools

import jax
import jax.numpy as jnp
from jax import lax
from jax.experimental import pallas as pl
from jax.experimental.pallas import tpu as pltpu
from jax.sharding import PartitionSpec as P

MESH = pl.DeviceIdType.MESH
TR_DEV = 2
TC_DEV = 32
SLOTS = 4
TILE = 512
EPS = 1e-06
NY, NZ, NX, NC = 4, 16, 4, 2

Z_STEP = [0] + [(q + 1) // 2 if q % 2 else -(q // 2) for q in range(1, NZ)]
Y_STEP = [(dy, p) for dy in (0, 1, 3, 2) for p in (0, 1)]
X_STEP = [(dx, dc) for dx in (0, 1, 3, 2) for dc in (0, 1)]
D_STEP = [0, 1, 3, 2]


def scaled(value, peak):
    return value / jnp.sqrt(value * peak + EPS)


def kernel(
    list_ref, count_ref, tiles_ref, row_out, col_out,
    tile, by_row, by_col, fold, z_src0, z_src, z_buf0, z_buf, meta_src, meta_y,
    y_src, y_buf, d_src, d_buf, f_src, f_buf, r_src, r_buf,
    load_sem, z_send, z_recv, m_send, m_recv, y_send, y_recv, d_send, d_recv,
    f_send, f_recv, r_send, r_recv,
):
    row, col = lax.axis_index("row"), lax.axis_index("col")
    y, z = row // NZ, lax.rem(row, NZ)
    x, core = col // NC, lax.rem(col, NC)
    half = lax.rem(z, 2)

    def z_peer(q):
        return (y * NZ + lax.rem(z + Z_STEP[q] + NZ, NZ), col)

    def y_peer(j):
        dy, p = Y_STEP[j]
        return (lax.rem(y + dy, NY) * NZ + (z + 1 - 2 * half if p else z), col)

    def x_peer(j):
        dx, dc = X_STEP[j]
        return (row, lax.rem(x + dx, NX) * NC + lax.rem(core + dc, NC))

    def d_peer(j):
        return (lax.rem(y + D_STEP[j], NY) * NZ + z, col)

    def remote(src, dst, send, recv, peer):
        return pltpu.make_async_remote_copy(
            src_ref=src, dst_ref=dst, send_sem=send, recv_sem=recv,
            device_id=peer, device_id_type=MESH,
        )

    barrier = pltpu.get_barrier_semaphore()
    peers = [z_peer(q) for q in range(NZ - 1, 0, -1)]
    peers += [y_peer(j) for j in range(7, 1, -1)]
    peers += [x_peer(j) for j in range(7, 0, -1)]
    for peer in peers:
        pl.semaphore_signal(barrier, inc=1, device_id=peer, device_id_type=MESH)

    loads = [
        pltpu.make_async_copy(tiles_ref.at[s], tile.at[s], load_sem.at[s]) for s in range(SLOTS)
    ]
    for load in loads:
        load.start()

    iota = lax.broadcasted_iota(jnp.int32, (8, 128), 0)
    tile_row = [list_ref[s, 0] - row * TR_DEV for s in range(SLOTS)]
    row_at = [jnp.clip(at, 0, TR_DEV - 1) for at in tile_row]
    live = [s < count_ref[0] for s in range(SLOTS)]
    meta = jnp.full((8, 128), -1.0, jnp.float32)
    for s in range(SLOTS):
        at = jnp.where(live[s], list_ref[s, 1] - col * TC_DEV, -1).astype(jnp.float32)
        meta = jnp.where(iota // 2 == s, jnp.full((8, 128), at), meta)
    meta_src[...] = meta
    for p in range(2):
        z_src0[p, 8:16, :] = meta
    in_row = [
        [jnp.where(live[s], jnp.where(tile_row[s] == t, 1.0, 0.0), 0.0) for t in range(TR_DEV)]
        for s in range(SLOTS)
    ]

    def combine(total):
        return (jnp.add, jnp.sum) if total else (jnp.maximum, jnp.max)

    def column_pass(k, weighted, total=False):
        join, fold_of = combine(total)
        for s in range(SLOTS):

            def body(c, acc):
                start = pl.multiple_of(c * 64, 64)
                weight = by_row[row_at[s], pl.ds(start, 64), :] if weighted else None
                acc = list(acc)
                for b in range(4):
                    part = jnp.abs(tile[s, pl.ds(start, 64), b * 128 : (b + 1) * 128])
                    if weighted:
                        part = part * weight
                    acc[b] = join(acc[b], fold_of(part.reshape(8, 8, 128), axis=0))
                return tuple(acc)

            zero = jnp.zeros((8, 128), jnp.float32)
            acc = lax.fori_loop(0, TILE // 64, body, (zero,) * 4)
            for b in range(4):
                line = fold_of(acc[b], axis=0, keepdims=True)
                at = 2 * s + b % 2
                which = half if b // 2 == 0 else 1 - half
                if k == 0:
                    z_src0[which, at : at + 1, :] = line
                else:
                    z_src[k - 1, which, at : at + 1, :] = line

    def row_pass(k, weighted, total=False):
        join, fold_of = combine(total)

        def body(blk, res):
            for sub in range(4):
                start = pl.multiple_of(blk * 128 + sub * 32, 32)
                sides = [jnp.zeros((32, 128), jnp.float32)] * TR_DEV
                for s in range(SLOTS):
                    part = None
                    for b in range(4):
                        piece = jnp.abs(tile[s, pl.ds(start, 32), b * 128 : (b + 1) * 128])
                        if weighted:
                            at = 2 * s + b % 2
                            piece = piece * by_col[b // 2, at : at + 1, :]
                        part = piece if part is None else join(part, piece)
                    sides = [
                        join(side, jnp.where(jnp.full((32, 128), in_row[s][t]) > 0.5, part, 0.0))
                        for t, side in enumerate(sides)
                    ]
                for t in range(TR_DEV):
                    fold[t, sub * 32 : (sub + 1) * 32, :] = sides[t]
            for t in range(TR_DEV):
                line = fold_of(fold[t].T, axis=0, keepdims=True)
                res = jnp.where(iota == t * 4 + blk, line, res)
            return res

        r_src[k] = lax.fori_loop(0, 4, body, jnp.zeros((8, 128), jnp.float32))

    def send_rows(k):
        for j in range(7, 0, -1):
            remote(r_src.at[k], r_buf.at[k, j], r_send.at[k], r_recv.at[k], x_peer(j)).start()

    def wait_rows(k, total=False):
        join, _ = combine(total)
        whole = r_buf.at[k, pl.ds(1, 7)]
        remote(whole, whole, r_send.at[k], r_recv.at[k], x_peer(1)).wait_recv()
        out = r_src[k]
        for j in range(1, 8):
            out = join(out, r_buf[k, j])
        return out

    def spread_rows(d):
        for t in range(TR_DEV):
            for blk in range(4):
                at = t * 4 + blk
                wide = jnp.broadcast_to(d[at : at + 1, :], (128, 128))
                by_row[t, blk * 128 : (blk + 1) * 128, :] = wide.T

    def spread_cols(e):
        for p in range(2):
            by_col[half if p == 0 else 1 - half] = e[p]

    def z_refs(k, q):
        if k == 0:
            return z_buf0.at[q]
        return z_buf.at[k - 1, q]

    def z_from(k, p):
        return z_src0.at[p] if k == 0 else z_src.at[k - 1, p]

    def send_z(k):
        for q in range(NZ - 1, 0, -1):
            remote(
                z_from(k, Z_STEP[q] % 2), z_refs(k, q), z_send.at[k], z_recv.at[k, q], z_peer(q)
            ).start()

    def gather_z(k, targets, wait, total=False):
        join, _ = combine(total)

        def add(acc, value, at):
            acc = list(acc)
            for turn in range(4):
                v = pltpu.roll(value, 2 * turn, 0) if turn else value
                m = pltpu.roll(at, 2 * turn, 0) if turn else at
                for j in range(8):
                    acc[j] = join(acc[j], jnp.where(m == targets[j], v, 0.0))
            return tuple(acc)

        def body(q, acc):
            if wait:
                ref = z_refs(k, q)
                remote(ref, ref, z_send.at[k], z_recv.at[k, q], z_peer(1)).wait_recv()
            value = z_buf0[q, 0:8, :] if k == 0 else z_buf[k - 1, q]
            return add(acc, value, z_buf0[q, 8:16, :])

        own = z_src0[0, 0:8, :] if k == 0 else z_src[k - 1, 0]
        acc = add((jnp.zeros((8, 128), jnp.float32),) * 8, own, meta_src[...])
        return lax.fori_loop(1, NZ, body, acc)

    def send_slots(k):
        own = []
        for j in range(1, 8):
            dy, p = Y_STEP[j]
            at = meta_y[Y_STEP.index(((NY - dy) % NY, p))]
            own.append(jnp.where(at < 0, -2.0, at))
        first = jnp.where(meta_src[...] < 0, -2.0, meta_src[...])
        acc = gather_z(k, [first] + own, True)
        for j in range(8):
            y_src[k, j] = acc[j]
        for j in range(7, 0, -1):
            remote(y_src.at[k, j], y_buf.at[k, j], y_send.at[k], y_recv.at[k], y_peer(j)).start()

    def wait_slots(k):
        whole = y_buf.at[k, pl.ds(1, 7)]
        remote(whole, whole, y_send.at[k], y_recv.at[k], y_peer(1)).wait_recv()
        out = [y_src[k, 0], y_buf[k, 1]]
        for j in range(2, 8):
            out[j % 2] = jnp.maximum(out[j % 2], y_buf[k, j])
        return out

    def send_dense(k, wait=False, total=False):
        every = [(4 * j + iota // 2).astype(jnp.float32) for j in range(8)]
        acc = gather_z(k, every, wait, total)
        for j in range(8):
            d_src[k, j] = acc[j]
        for j in range(3, 0, -1):
            there = lax.rem(y + D_STEP[j], NY)
            remote(
                d_src.at[k, pl.ds(2 * there, 2)], d_buf.at[k, j], d_send.at[k], d_recv.at[k],
                d_peer(j),
            ).start()

    def wait_dense(k, total=False):
        join, _ = combine(total)
        whole = d_buf.at[k, pl.ds(1, 3)]
        remote(whole, whole, d_send.at[k], d_recv.at[k], d_peer(1)).wait_recv()
        out = d_src[k, pl.ds(2 * y, 2)]
        for j in range(1, 4):
            out = join(out, d_buf[k, j])
        return out

    for load in loads:
        load.wait()
    row_pass(0, False)
    column_pass(0, False)
    pl.semaphore_wait(barrier, len(peers))
    send_rows(0)
    send_z(0)
    for j in range(7, 0, -1):
        remote(meta_src, meta_y.at[j], m_send, m_recv, y_peer(j)).start()

    one = jnp.ones((8, 128), jnp.float32)
    d1 = scaled(one, wait_rows(0))
    spread_rows(d1)
    column_pass(1, True)
    send_z(1)

    whole = meta_y.at[pl.ds(1, 7)]
    remote(whole, whole, m_send, m_recv, y_peer(1)).wait_recv()
    send_slots(0)
    send_dense(0)
    send_slots(1)
    e1 = [scaled(one, peak) for peak in wait_slots(0)]
    spread_cols(e1)
    row_pass(1, True)
    send_rows(1)
    send_dense(1)
    e2 = [scaled(e, peak) for e, peak in zip(e1, wait_slots(1))]
    spread_cols(e2)
    row_pass(2, True)
    send_rows(2)
    d2 = scaled(d1, wait_rows(1))
    spread_rows(d2)
    column_pass(2, True)
    send_z(2)
    d3 = scaled(d2, wait_rows(2))
    spread_rows(d3)
    column_pass(3, True, total=True)
    send_z(3)
    send_slots(2)
    send_dense(2)
    send_dense(3, wait=True, total=True)
    e3 = [scaled(e, peak) for e, peak in zip(e2, wait_slots(2))]
    spread_cols(e3)
    row_pass(3, True, total=True)
    send_rows(3)

    dense = jnp.ones((2, 8, 128), jnp.float32)
    for k in range(3):
        dense = scaled(dense, wait_dense(k))
    f_src[...] = scaled(dense, wait_dense(3, total=True))
    for j in range(7, 0, -1):
        remote(f_src, f_buf.at[j], f_send, f_recv, y_peer(j)).start()
    row_out[...] = scaled(d3, wait_rows(3, total=True))
    whole = f_buf.at[pl.ds(1, 7)]
    remote(whole, whole, f_send, f_recv, y_peer(1)).wait_recv()
    for g in range(4):
        dy = Y_STEP[2 * g][0]
        there = lax.rem(y - dy + NY, NY)
        for n in range(2):
            near = f_src[n] if g == 0 else f_buf[2 * g, n]
            far = f_buf[2 * g + 1, n]
            low = jnp.where(half == 0, near, far)
            high = jnp.where(half == 0, far, near)
            for s in range(4):
                at = (s % 2) * 4
                col_out[there * 4 + n * 2 + s // 2, at : at + 2, :] = low[2 * s : 2 * s + 2, :]
                col_out[there * 4 + n * 2 + s // 2, at + 2 : at + 4, :] = high[2 * s : 2 * s + 2, :]

    for k in range(4):
        ref = z_buf0.at[pl.ds(1, 15)] if k == 0 else z_buf.at[k - 1, pl.ds(1, 15)]
        remote(ref, ref, z_send.at[k], z_recv.at[k, 1], z_peer(1)).wait_send()
        ref = r_buf.at[k, pl.ds(1, 7)]
        remote(ref, ref, r_send.at[k], r_recv.at[k], x_peer(1)).wait_send()
        ref = d_buf.at[k, pl.ds(1, 3)]
        remote(ref, ref, d_send.at[k], d_recv.at[k], d_peer(1)).wait_send()
    for k in range(3):
        ref = y_buf.at[k, pl.ds(1, 7)]
        remote(ref, ref, y_send.at[k], y_recv.at[k], y_peer(1)).wait_send()
    ref = meta_y.at[pl.ds(1, 7)]
    remote(ref, ref, m_send, m_recv, y_peer(1)).wait_send()
    ref = f_buf.at[pl.ds(1, 7)]
    remote(ref, ref, f_send, f_recv, y_peer(1)).wait_send()


def on_device(tiles, tile_list, tile_count):
    f32 = jnp.float32
    dma = pltpu.SemaphoreType.DMA
    row_scale, col_scale = pl.pallas_call(
        kernel,
        out_shape=(
            jax.ShapeDtypeStruct((8, 128), f32),
            jax.ShapeDtypeStruct((16, 8, 128), f32),
        ),
        in_specs=[
            pl.BlockSpec(memory_space=pltpu.SMEM),
            pl.BlockSpec(memory_space=pltpu.SMEM),
            pl.BlockSpec(memory_space=pl.ANY),
        ],
        out_specs=(
            pl.BlockSpec(memory_space=pltpu.VMEM),
            pl.BlockSpec(memory_space=pltpu.VMEM),
        ),
        scratch_shapes=[
            pltpu.VMEM((SLOTS, TILE, TILE), f32),
            pltpu.VMEM((TR_DEV, TILE, 128), f32),
            pltpu.VMEM((2, 8, 128), f32),
            pltpu.VMEM((TR_DEV, 128, 128), f32),
            pltpu.VMEM((2, 16, 128), f32),
            pltpu.VMEM((3, 2, 8, 128), f32),
            pltpu.VMEM((NZ, 16, 128), f32),
            pltpu.VMEM((3, NZ, 8, 128), f32),
            pltpu.VMEM((8, 128), f32),
            pltpu.VMEM((8, 8, 128), f32),
            pltpu.VMEM((3, 8, 8, 128), f32),
            pltpu.VMEM((3, 8, 8, 128), f32),
            pltpu.VMEM((4, 8, 8, 128), f32),
            pltpu.VMEM((4, 4, 2, 8, 128), f32),
            pltpu.VMEM((2, 8, 128), f32),
            pltpu.VMEM((8, 2, 8, 128), f32),
            pltpu.VMEM((4, 8, 128), f32),
            pltpu.VMEM((4, 8, 8, 128), f32),
            dma((SLOTS,)),
            dma((4,)),
            dma((4, NZ)),
            dma,
            dma,
            dma((3,)),
            dma((3,)),
            dma((4,)),
            dma((4,)),
            dma,
            dma,
            dma((4,)),
            dma((4,)),
        ],
        compiler_params=pltpu.CompilerParams(
            collective_id=0, has_side_effects=True, vmem_limit_bytes=24 * 1024 * 1024
        ),
    )(tile_list, tile_count, tiles)
    return row_scale.reshape(-1), col_scale.reshape(-1)


def solution(mesh):
    return jax.shard_map(
        on_device,
        mesh=mesh,
        in_specs=(P(("row", "col"), None, None), P(("row", "col"), None), P(("row", "col"))),
        out_specs=(P("row"), P("col")),
        check_vma=False,
    )
```

```python
import functools

import jax
import jax.numpy as jnp
from jax import lax
from jax.experimental import pallas as pl
from jax.experimental.pallas import tpu as pltpu
from jax.sharding import PartitionSpec as P

MESH = pl.DeviceIdType.MESH
TR_DEV = 2
TC_DEV = 32
SLOTS = 4
TILE = 512
EPS = 1e-06
NY, NZ, NX, NC = 4, 16, 4, 2

Z_STEP = [0] + [(q + 1) // 2 if q % 2 else -(q // 2) for q in range(1, NZ)]
Y_STEP = [(dy, p) for dy in (0, 1, 3, 2) for p in (0, 1)]
X_STEP = [(dx, dc) for dx in (0, 1, 3, 2) for dc in (0, 1)]
D_STEP = [0, 1, 3, 2]


def scaled(value, peak):
    return value / jnp.sqrt(value * peak + EPS)


def kernel(
    list_ref, count_ref, tiles_ref, row_out, col_out,
    tile, by_row, by_col, fold, z_src0, z_src, z_buf0, z_buf, meta_src, meta_y, meta_z,
    y_src, y_buf, d_src, d_buf, f_src, f_buf, g_src, g_buf, r_src, r_buf,
    load_sem, z_send, z_recv, m_send, m_recv, y_send, y_recv, d_send, d_recv,
    f_send, f_recv, g_send, g_recv, r_send, r_recv,
):
    row, col = lax.axis_index("row"), lax.axis_index("col")
    y, z = row // NZ, lax.rem(row, NZ)
    x, core = col // NC, lax.rem(col, NC)
    half = lax.rem(z, 2)

    def z_peer(q):
        return (y * NZ + lax.rem(z + Z_STEP[q] + NZ, NZ), col)

    def y_peer(j):
        dy, p = Y_STEP[j]
        return (lax.rem(y + dy, NY) * NZ + (z + 1 - 2 * half if p else z), col)

    def x_peer(j):
        dx, dc = X_STEP[j]
        return (row, lax.rem(x + dx, NX) * NC + lax.rem(core + dc, NC))

    def d_peer(j):
        return (lax.rem(y + D_STEP[j], NY) * NZ + z, col)

    def remote(src, dst, send, recv, peer):
        return pltpu.make_async_remote_copy(
            src_ref=src, dst_ref=dst, send_sem=send, recv_sem=recv,
            device_id=peer, device_id_type=MESH,
        )

    barrier = pltpu.get_barrier_semaphore()
    peers = [z_peer(q) for q in range(NZ - 1, 0, -1)]
    peers += [y_peer(j) for j in range(7, 1, -1)]
    peers += [x_peer(j) for j in range(7, 0, -1)]
    for peer in peers:
        pl.semaphore_signal(barrier, inc=1, device_id=peer, device_id_type=MESH)

    loads = [
        pltpu.make_async_copy(tiles_ref.at[s], tile.at[s], load_sem.at[s]) for s in range(SLOTS)
    ]
    for load in loads:
        load.start()

    iota = lax.broadcasted_iota(jnp.int32, (8, 128), 0)
    tile_row = [list_ref[0, s] - row * TR_DEV for s in range(SLOTS)]
    row_at = [jnp.clip(at, 0, TR_DEV - 1) for at in tile_row]
    live = [s < count_ref[0] for s in range(SLOTS)]
    lane = lax.broadcasted_iota(jnp.int32, (8, 128), 1)
    meta = jnp.full((8, 128), -1.0, jnp.float32)
    meta_line = jnp.full((1, 128), -1.0, jnp.float32)
    for s in range(SLOTS):
        at = jnp.where(live[s], list_ref[1, s] - col * TC_DEV, -1).astype(jnp.float32)
        meta = jnp.where(iota // 2 == s, jnp.full((8, 128), at), meta)
        meta_line = jnp.where(lane[0:1] // 2 == s, jnp.full((1, 128), at), meta_line)
    meta_src[...] = meta
    for p in range(2):
        z_src0[p, 8:9, :] = meta_line
    in_row = [
        [jnp.where(live[s], jnp.where(tile_row[s] == t, 1.0, 0.0), 0.0) for t in range(TR_DEV)]
        for s in range(SLOTS)
    ]

    def combine(total):
        return (jnp.add, jnp.sum) if total else (jnp.maximum, jnp.max)

    def put_columns(k, s, acc, fold_of):
        for b in range(4):
            line = fold_of(acc[b], axis=0, keepdims=True)
            at = 2 * s + b % 2
            which = half if b // 2 == 0 else 1 - half
            if k == 0:
                z_src0[which, at : at + 1, :] = line
            else:
                z_src[k - 1, which, at : at + 1, :] = line

    def put_rows(k, fold_of):
        res = jnp.zeros((8, 128), jnp.float32)
        for t in range(TR_DEV):
            for blk in range(4):
                line = fold_of(fold[t, blk * 128 : (blk + 1) * 128, :].T, axis=0, keepdims=True)
                res = jnp.where(iota == t * 4 + blk, line, res)
        r_src[k] = res

    zeros = (jnp.zeros((8, 128), jnp.float32),) * 4

    def first_pass():
        for s in range(SLOTS):
            loads[s].wait()

            def body(c, acc):
                start = pl.multiple_of(c * 32, 32)
                acc, part = list(acc), None
                for b in range(4):
                    piece = jnp.abs(tile[s, pl.ds(start, 32), b * 128 : (b + 1) * 128])
                    tile[s, pl.ds(start, 32), b * 128 : (b + 1) * 128] = piece
                    acc[b] = jnp.maximum(acc[b], jnp.max(piece.reshape(4, 8, 128), axis=0))
                    part = piece if part is None else jnp.maximum(part, piece)
                for t in range(TR_DEV):
                    side = jnp.where(jnp.full((32, 128), in_row[s][t]) > 0.5, part, 0.0)
                    if s:
                        side = jnp.maximum(side, fold[t, pl.ds(start, 32), :])
                    fold[t, pl.ds(start, 32), :] = side
                return tuple(acc)

            put_columns(0, s, lax.fori_loop(0, TILE // 32, body, zeros, unroll=2), jnp.max)
        put_rows(0, jnp.max)

    def column_pass(k, total=False):
        join, fold_of = combine(total)
        accs = []
        for s in range(SLOTS):

            def body(c, acc):
                start = pl.multiple_of(c * 64, 64)
                weight = by_row[row_at[s], pl.ds(start, 64), :]
                acc = list(acc)
                for b in range(4):
                    part = tile[s, pl.ds(start, 64), b * 128 : (b + 1) * 128] * weight
                    acc[b] = join(acc[b], fold_of(part.reshape(8, 8, 128), axis=0))
                return tuple(acc)

            accs.append(lax.fori_loop(0, TILE // 64, body, zeros, unroll=4))
        for s in range(SLOTS):
            put_columns(k, s, accs[s], fold_of)

    def row_pass(k, total=False):
        join, fold_of = combine(total)

        def body(c, carry):
            start = pl.multiple_of(c * 32, 32)
            sides = [jnp.zeros((32, 128), jnp.float32)] * TR_DEV
            for s in range(SLOTS):
                part = None
                for b in range(4):
                    at = 2 * s + b % 2
                    piece = tile[s, pl.ds(start, 32), b * 128 : (b + 1) * 128]
                    piece = piece * by_col[b // 2, at : at + 1, :]
                    part = piece if part is None else join(part, piece)
                sides = [
                    join(side, jnp.where(jnp.full((32, 128), in_row[s][t]) > 0.5, part, 0.0))
                    for t, side in enumerate(sides)
                ]
            for t in range(TR_DEV):
                fold[t, pl.ds(start, 32), :] = sides[t]
            return carry

        lax.fori_loop(0, TILE // 32, body, 0, unroll=2)
        put_rows(k, fold_of)

    def send_rows(k):
        for j in range(7, 0, -1):
            remote(r_src.at[k], r_buf.at[k, j], r_send.at[k], r_recv.at[k], x_peer(j)).start()

    def wait_rows(k, total=False):
        join, _ = combine(total)
        whole = r_buf.at[k, pl.ds(1, 7)]
        remote(whole, whole, r_send.at[k], r_recv.at[k], x_peer(1)).wait_recv()
        out = r_src[k]
        for j in range(1, 8):
            out = join(out, r_buf[k, j])
        return out

    def spread_rows(d):
        for t in range(TR_DEV):
            for blk in range(4):
                at = t * 4 + blk
                wide = jnp.broadcast_to(d[at : at + 1, :], (128, 128))
                by_row[t, blk * 128 : (blk + 1) * 128, :] = wide.T

    def spread_cols(e):
        for p in range(2):
            by_col[half if p == 0 else 1 - half] = e[p]

    def z_refs(k, q):
        if k == 0:
            return z_buf0.at[q]
        return z_buf.at[k - 1, q]

    def z_from(k, p):
        return z_src0.at[p] if k == 0 else z_src.at[k - 1, p]

    def send_z(k):
        for q in range(NZ - 1, 0, -1):
            remote(
                z_from(k, Z_STEP[q] % 2), z_refs(k, q), z_send.at[k], z_recv.at[k, q], z_peer(q)
            ).start()

    def gather_z(k, targets, wait, total=False):
        join, _ = combine(total)

        def add(acc, value, at):
            acc = list(acc)
            for turn in range(4):
                v = pltpu.roll(value, 2 * turn, 0) if turn else value
                m = pltpu.roll(at, 2 * turn, 0) if turn else at
                for j in range(8):
                    acc[j] = join(acc[j], jnp.where(m == targets[j], v, 0.0))
            return tuple(acc)

        def body(q, acc):
            if wait:
                ref = z_refs(k, q)
                remote(ref, ref, z_send.at[k], z_recv.at[k, q], z_peer(1)).wait_recv()
            value = z_buf0[q, 0:8, :] if k == 0 else z_buf[k - 1, q]
            if k == 0 and wait:
                line = jnp.where(lane == iota, z_buf0[q, 8:9, :], -1.0)
                at = jnp.broadcast_to(jnp.max(line, axis=1, keepdims=True), (8, 128))
                meta_z[q] = at
            else:
                at = meta_z[q]
            return add(acc, value, at)

        own = z_src0[0, 0:8, :] if k == 0 else z_src[k - 1, 0]
        acc = add((jnp.zeros((8, 128), jnp.float32),) * 8, own, meta_src[...])
        return lax.fori_loop(1, NZ, body, acc)

    def send_slots(k):
        own = []
        for j in range(1, 8):
            dy, p = Y_STEP[j]
            at = meta_y[Y_STEP.index(((NY - dy) % NY, p))]
            own.append(jnp.where(at < 0, -2.0, at))
        first = jnp.where(meta_src[...] < 0, -2.0, meta_src[...])
        acc = gather_z(k, [first] + own, True)
        for j in range(8):
            y_src[k, j] = acc[j]
        for j in range(7, 0, -1):
            remote(y_src.at[k, j], y_buf.at[k, j], y_send.at[k], y_recv.at[k], y_peer(j)).start()

    def wait_slots(k):
        whole = y_buf.at[k, pl.ds(1, 7)]
        remote(whole, whole, y_send.at[k], y_recv.at[k], y_peer(1)).wait_recv()
        out = [y_src[k, 0], y_buf[k, 1]]
        for j in range(2, 8):
            out[j % 2] = jnp.maximum(out[j % 2], y_buf[k, j])
        return out

    def dense(k, wait=False, total=False):
        every = [(4 * j + iota // 2).astype(jnp.float32) for j in range(8)]
        return gather_z(k, every, wait, total)

    def send_dense(k):
        for j, acc in enumerate(dense(k)):
            d_src[k, j] = acc
        for j in range(3, 0, -1):
            there = lax.rem(y + D_STEP[j], NY)
            remote(
                d_src.at[k, pl.ds(2 * there, 2)], d_buf.at[k, j], d_send.at[k], d_recv.at[k],
                d_peer(j),
            ).start()

    def send_totals():
        for j, acc in enumerate(dense(3, wait=True, total=True)):
            g_src[j] = acc
        for j in range(7, 0, -1):
            remote(g_src, g_buf.at[j], g_send, g_recv, y_peer(j)).start()

    def wait_dense(k):
        whole = d_buf.at[k, pl.ds(1, 3)]
        remote(whole, whole, d_send.at[k], d_recv.at[k], d_peer(1)).wait_recv()
        out = d_src[k, pl.ds(2 * y, 2)]
        for j in range(1, 4):
            out = jnp.maximum(out, d_buf[k, j])
        return out

    first_pass()
    pl.semaphore_wait(barrier, len(peers))
    send_rows(0)
    send_z(0)
    for j in range(7, 0, -1):
        remote(meta_src, meta_y.at[j], m_send, m_recv, y_peer(j)).start()

    one = jnp.ones((8, 128), jnp.float32)
    d1 = scaled(one, wait_rows(0))
    spread_rows(d1)
    column_pass(1)
    send_z(1)

    whole = meta_y.at[pl.ds(1, 7)]
    remote(whole, whole, m_send, m_recv, y_peer(1)).wait_recv()
    send_slots(0)
    send_dense(0)
    send_slots(1)
    e1 = [scaled(one, peak) for peak in wait_slots(0)]
    spread_cols(e1)
    row_pass(1)
    send_rows(1)
    send_dense(1)
    e2 = [scaled(e, peak) for e, peak in zip(e1, wait_slots(1))]
    spread_cols(e2)
    row_pass(2)
    send_rows(2)
    d2 = scaled(d1, wait_rows(1))
    spread_rows(d2)
    column_pass(2)
    send_z(2)
    d3 = scaled(d2, wait_rows(2))
    spread_rows(d3)
    column_pass(3, total=True)
    send_z(3)
    send_slots(2)
    send_dense(2)
    send_totals()
    mine = jnp.ones((2, 8, 128), jnp.float32)
    for k in range(3):
        mine = scaled(mine, wait_dense(k))
    f_src[...] = mine
    for j in range(7, 0, -1):
        remote(f_src, f_buf.at[j], f_send, f_recv, y_peer(j)).start()
    e3 = [scaled(e, peak) for e, peak in zip(e2, wait_slots(2))]
    spread_cols(e3)
    row_pass(3, total=True)
    send_rows(3)

    row_out[...] = scaled(d3, wait_rows(3, total=True))
    whole = f_buf.at[pl.ds(1, 7)]
    remote(whole, whole, f_send, f_recv, y_peer(1)).wait_recv()
    whole = g_buf.at[pl.ds(1, 7)]
    remote(whole, whole, g_send, g_recv, y_peer(1)).wait_recv()
    for g in range(4):
        dy = Y_STEP[2 * g][0]
        there = lax.rem(y - dy + NY, NY)
        for n in range(2):
            at = 2 * there + n
            sums = [g_src[at], g_buf[1, at]]
            for j in range(2, 8):
                sums[j % 2] = sums[j % 2] + g_buf[j, at]
            near = scaled(f_src[n] if g == 0 else f_buf[2 * g, n], sums[0])
            far = scaled(f_buf[2 * g + 1, n], sums[1])
            low = jnp.where(half == 0, near, far)
            high = jnp.where(half == 0, far, near)
            for s in range(4):
                at = (s % 2) * 4
                col_out[there * 4 + n * 2 + s // 2, at : at + 2, :] = low[2 * s : 2 * s + 2, :]
                col_out[there * 4 + n * 2 + s // 2, at + 2 : at + 4, :] = high[2 * s : 2 * s + 2, :]

    for k in range(4):
        ref = z_buf0.at[pl.ds(1, 15)] if k == 0 else z_buf.at[k - 1, pl.ds(1, 15)]
        remote(ref, ref, z_send.at[k], z_recv.at[k, 1], z_peer(1)).wait_send()
        ref = r_buf.at[k, pl.ds(1, 7)]
        remote(ref, ref, r_send.at[k], r_recv.at[k], x_peer(1)).wait_send()
    for k in range(3):
        ref = d_buf.at[k, pl.ds(1, 3)]
        remote(ref, ref, d_send.at[k], d_recv.at[k], d_peer(1)).wait_send()
        ref = y_buf.at[k, pl.ds(1, 7)]
        remote(ref, ref, y_send.at[k], y_recv.at[k], y_peer(1)).wait_send()
    ref = meta_y.at[pl.ds(1, 7)]
    remote(ref, ref, m_send, m_recv, y_peer(1)).wait_send()
    ref = f_buf.at[pl.ds(1, 7)]
    remote(ref, ref, f_send, f_recv, y_peer(1)).wait_send()
    ref = g_buf.at[pl.ds(1, 7)]
    remote(ref, ref, g_send, g_recv, y_peer(1)).wait_send()


def on_device(tiles, tile_list, tile_count):
    f32 = jnp.float32
    dma = pltpu.SemaphoreType.DMA
    row_scale, col_scale = pl.pallas_call(
        kernel,
        out_shape=(
            jax.ShapeDtypeStruct((8, 128), f32),
            jax.ShapeDtypeStruct((16, 8, 128), f32),
        ),
        in_specs=[
            pl.BlockSpec(memory_space=pltpu.SMEM),
            pl.BlockSpec(memory_space=pltpu.SMEM),
            pl.BlockSpec(memory_space=pltpu.HBM),
        ],
        out_specs=(
            pl.BlockSpec(memory_space=pltpu.VMEM),
            pl.BlockSpec(memory_space=pltpu.VMEM),
        ),
        scratch_shapes=[
            pltpu.VMEM((SLOTS, TILE, TILE), f32),
            pltpu.VMEM((TR_DEV, TILE, 128), f32),
            pltpu.VMEM((2, 8, 128), f32),
            pltpu.VMEM((TR_DEV, TILE, 128), f32),
            pltpu.VMEM((2, 9, 128), f32),
            pltpu.VMEM((3, 2, 8, 128), f32),
            pltpu.VMEM((NZ, 9, 128), f32),
            pltpu.VMEM((3, NZ, 8, 128), f32),
            pltpu.VMEM((8, 128), f32),
            pltpu.VMEM((8, 8, 128), f32),
            pltpu.VMEM((NZ, 8, 128), f32),
            pltpu.VMEM((3, 8, 8, 128), f32),
            pltpu.VMEM((3, 8, 8, 128), f32),
            pltpu.VMEM((3, 8, 8, 128), f32),
            pltpu.VMEM((3, 4, 2, 8, 128), f32),
            pltpu.VMEM((2, 8, 128), f32),
            pltpu.VMEM((8, 2, 8, 128), f32),
            pltpu.VMEM((8, 8, 128), f32),
            pltpu.VMEM((8, 8, 8, 128), f32),
            pltpu.VMEM((4, 8, 128), f32),
            pltpu.VMEM((4, 8, 8, 128), f32),
            dma((SLOTS,)),
            dma((4,)),
            dma((4, NZ)),
            dma,
            dma,
            dma((3,)),
            dma((3,)),
            dma((3,)),
            dma((3,)),
            dma,
            dma,
            dma,
            dma,
            dma((4,)),
            dma((4,)),
        ],
        compiler_params=pltpu.CompilerParams(
            collective_id=0, has_side_effects=True, vmem_limit_bytes=52 * 1024 * 1024
        ),
    )(tile_list.T, tile_count, tiles)
    return row_scale.reshape(-1), col_scale.reshape(-1)


def solution(mesh):
    return jax.shard_map(
        on_device,
        mesh=mesh,
        in_specs=(P(("row", "col"), None, None), P(("row", "col"), None), P(("row", "col"))),
        out_specs=(P("row"), P("col")),
        check_vma=False,
    )
```

```python
import functools

import jax
import jax.numpy as jnp
from jax import lax
from jax.experimental import pallas as pl
from jax.experimental.pallas import tpu as pltpu
from jax.sharding import PartitionSpec as P

MESH = pl.DeviceIdType.MESH
TR_DEV = 2
TC_DEV = 32
SLOTS = 4
TILE = 512
EPS = 1e-06
NY, NZ, NX, NC = 4, 16, 4, 2

Z_STEP = [0] + [(q + 1) // 2 if q % 2 else -(q // 2) for q in range(1, NZ)]
Y_STEP = [(dy, p) for dy in (0, 1, 3, 2) for p in (0, 1)]
X_STEP = [(dx, dc) for dx in (0, 1, 3, 2) for dc in (0, 1)]
D_STEP = [0, 1, 3, 2]


def scaled(value, peak):
    return value / jnp.sqrt(value * peak + EPS)


def kernel(
    facts_ref, tiles_ref, row_out, col_out,
    tile, by_row, by_col, fold, z_src0, z_src, z_buf0, z_buf, meta_src, meta_y, meta_z,
    y_src, y_buf, d_src, d_buf, f_src, f_buf, g_src, g_buf, r_src, r_buf,
    load_sem, z_send, z_recv, m_send, m_recv, y_send, y_recv, d_send, d_recv,
    f_send, f_recv, g_send, g_recv, r_send, r_recv,
):
    row, col = lax.axis_index("row"), lax.axis_index("col")
    y, z = row // NZ, lax.rem(row, NZ)
    x, core = col // NC, lax.rem(col, NC)
    half = lax.rem(z, 2)

    def z_peer(q):
        return (y * NZ + lax.rem(z + Z_STEP[q] + NZ, NZ), col)

    def y_peer(j):
        dy, p = Y_STEP[j]
        return (lax.rem(y + dy, NY) * NZ + (z + 1 - 2 * half if p else z), col)

    def x_peer(j):
        dx, dc = X_STEP[j]
        return (row, lax.rem(x + dx, NX) * NC + lax.rem(core + dc, NC))

    def d_peer(j):
        return (lax.rem(y + D_STEP[j], NY) * NZ + z, col)

    def remote(src, dst, send, recv, peer):
        return pltpu.make_async_remote_copy(
            src_ref=src, dst_ref=dst, send_sem=send, recv_sem=recv,
            device_id=peer, device_id_type=MESH,
        )

    barrier = pltpu.get_barrier_semaphore()
    peers = [z_peer(q) for q in range(NZ - 1, 0, -1)]
    peers += [y_peer(j) for j in range(7, 1, -1)]
    peers += [x_peer(j) for j in range(7, 0, -1)]
    for peer in peers:
        pl.semaphore_signal(barrier, inc=1, device_id=peer, device_id_type=MESH)

    loads = [
        pltpu.make_async_copy(tiles_ref.at[s], tile.at[s], load_sem.at[s]) for s in range(SLOTS)
    ]
    for load in loads:
        load.start()

    iota = lax.broadcasted_iota(jnp.int32, (8, 128), 0)
    lane = lax.broadcasted_iota(jnp.int32, (8, 128), 1)

    def wide(value):
        return jnp.broadcast_to(value, (8, 128))

    def tall(value, rows):
        return jnp.broadcast_to(value[None], (rows // 8, 8, 128)).reshape(rows, 128)

    second, in_row = [], []
    meta = jnp.full((8, 128), -1.0, jnp.float32)
    meta_line = jnp.full((1, 128), -1.0, jnp.float32)
    for s in range(SLOTS):
        tile_row = wide(facts_ref[0:1, s : s + 1])
        live = tile_row >= 0
        tile_row = tile_row - row * TR_DEV
        second.append(jnp.where(tile_row > 0, 1.0, 0.0))
        in_row.append(
            [jnp.where(live, jnp.where(tile_row == t, 1.0, 0.0), 0.0) for t in range(TR_DEV)]
        )
        at = jnp.where(live, wide(facts_ref[1:2, s : s + 1]) - col * TC_DEV, -1)
        at = at.astype(jnp.float32)
        meta = jnp.where(iota // 2 == s, at, meta)
        meta_line = jnp.where(lane[0:1] // 2 == s, at[0:1], meta_line)
    meta_src[...] = meta
    for p in range(2):
        z_src0[p, 8:9, :] = meta_line

    def combine(total):
        return (jnp.add, jnp.sum) if total else (jnp.maximum, jnp.max)

    def put_columns(k, s, acc, fold_of):
        for b in range(4):
            line = fold_of(acc[b], axis=0, keepdims=True)
            at = 2 * s + b % 2
            which = half if b // 2 == 0 else 1 - half
            if k == 0:
                z_src0[which, at : at + 1, :] = line
            else:
                z_src[k - 1, which, at : at + 1, :] = line

    def put_rows(k, fold_of):
        res = jnp.zeros((8, 128), jnp.float32)
        for t in range(TR_DEV):
            for blk in range(4):
                line = fold_of(fold[t, blk * 128 : (blk + 1) * 128, :].T, axis=0, keepdims=True)
                res = jnp.where(iota == t * 4 + blk, line, res)
        r_src[k] = res

    zeros = (jnp.zeros((8, 128), jnp.float32),) * 4

    def first_pass():
        for s in range(SLOTS):
            loads[s].wait()

            def body(c, acc):
                start = pl.multiple_of(c * 32, 32)
                acc, part = list(acc), None
                for b in range(4):
                    piece = jnp.abs(tile[s, pl.ds(start, 32), b * 128 : (b + 1) * 128])
                    tile[s, pl.ds(start, 32), b * 128 : (b + 1) * 128] = piece
                    acc[b] = jnp.maximum(acc[b], jnp.max(piece.reshape(4, 8, 128), axis=0))
                    part = piece if part is None else jnp.maximum(part, piece)
                for t in range(TR_DEV):
                    side = jnp.where(tall(in_row[s][t], 32) > 0.5, part, 0.0)
                    if s:
                        side = jnp.maximum(side, fold[t, pl.ds(start, 32), :])
                    fold[t, pl.ds(start, 32), :] = side
                return tuple(acc)

            put_columns(0, s, lax.fori_loop(0, TILE // 32, body, zeros, unroll=2), jnp.max)
        put_rows(0, jnp.max)

    def column_pass(k, total=False):
        join, fold_of = combine(total)
        accs = []
        for s in range(SLOTS):

            def body(c, acc):
                start = pl.multiple_of(c * 64, 64)
                weight = jnp.where(
                    tall(second[s], 64) > 0.5,
                    by_row[1, pl.ds(start, 64), :],
                    by_row[0, pl.ds(start, 64), :],
                )
                acc = list(acc)
                for b in range(4):
                    part = tile[s, pl.ds(start, 64), b * 128 : (b + 1) * 128] * weight
                    acc[b] = join(acc[b], fold_of(part.reshape(8, 8, 128), axis=0))
                return tuple(acc)

            accs.append(lax.fori_loop(0, TILE // 64, body, zeros, unroll=4))
        for s in range(SLOTS):
            put_columns(k, s, accs[s], fold_of)

    def row_pass(k, total=False):
        join, fold_of = combine(total)

        def body(c, carry):
            start = pl.multiple_of(c * 32, 32)
            sides = [jnp.zeros((32, 128), jnp.float32)] * TR_DEV
            for s in range(SLOTS):
                part = None
                for b in range(4):
                    at = 2 * s + b % 2
                    piece = tile[s, pl.ds(start, 32), b * 128 : (b + 1) * 128]
                    piece = piece * by_col[b // 2, at : at + 1, :]
                    part = piece if part is None else join(part, piece)
                sides = [
                    join(side, jnp.where(tall(in_row[s][t], 32) > 0.5, part, 0.0))
                    for t, side in enumerate(sides)
                ]
            for t in range(TR_DEV):
                fold[t, pl.ds(start, 32), :] = sides[t]
            return carry

        lax.fori_loop(0, TILE // 32, body, 0, unroll=2)
        put_rows(k, fold_of)

    def send_rows(k):
        for j in range(7, 0, -1):
            remote(r_src.at[k], r_buf.at[k, j], r_send.at[k], r_recv.at[k], x_peer(j)).start()

    def wait_rows(k, total=False):
        join, _ = combine(total)
        whole = r_buf.at[k, pl.ds(1, 7)]
        remote(whole, whole, r_send.at[k], r_recv.at[k], x_peer(1)).wait_recv()
        out = r_src[k]
        for j in range(1, 8):
            out = join(out, r_buf[k, j])
        return out

    def spread_rows(d):
        for t in range(TR_DEV):
            for blk in range(4):
                at = t * 4 + blk
                wide = jnp.broadcast_to(d[at : at + 1, :], (128, 128))
                by_row[t, blk * 128 : (blk + 1) * 128, :] = wide.T

    def spread_cols(e):
        for p in range(2):
            by_col[half if p == 0 else 1 - half] = e[p]

    def z_refs(k, q):
        if k == 0:
            return z_buf0.at[q]
        return z_buf.at[k - 1, q]

    def z_from(k, p):
        return z_src0.at[p] if k == 0 else z_src.at[k - 1, p]

    def send_z(k):
        for q in range(NZ - 1, 0, -1):
            remote(
                z_from(k, Z_STEP[q] % 2), z_refs(k, q), z_send.at[k], z_recv.at[k, q], z_peer(q)
            ).start()

    def gather_z(k, targets, wait, total=False):
        join, _ = combine(total)

        def add(acc, value, at):
            acc = list(acc)
            for turn in range(4):
                v = pltpu.roll(value, 2 * turn, 0) if turn else value
                m = pltpu.roll(at, 2 * turn, 0) if turn else at
                for j in range(8):
                    acc[j] = join(acc[j], jnp.where(m == targets[j], v, 0.0))
            return tuple(acc)

        def body(q, acc):
            if wait:
                ref = z_refs(k, q)
                remote(ref, ref, z_send.at[k], z_recv.at[k, q], z_peer(1)).wait_recv()
            value = z_buf0[q, 0:8, :] if k == 0 else z_buf[k - 1, q]
            if k == 0 and wait:
                line = jnp.where(lane == iota, z_buf0[q, 8:9, :], -1.0)
                at = jnp.broadcast_to(jnp.max(line, axis=1, keepdims=True), (8, 128))
                meta_z[q] = at
            else:
                at = meta_z[q]
            return add(acc, value, at)

        own = z_src0[0, 0:8, :] if k == 0 else z_src[k - 1, 0]
        acc = add((jnp.zeros((8, 128), jnp.float32),) * 8, own, meta_src[...])
        return lax.fori_loop(1, NZ, body, acc)

    def send_slots(k):
        own = []
        for j in range(1, 8):
            dy, p = Y_STEP[j]
            at = meta_y[Y_STEP.index(((NY - dy) % NY, p))]
            own.append(jnp.where(at < 0, -2.0, at))
        first = jnp.where(meta_src[...] < 0, -2.0, meta_src[...])
        acc = gather_z(k, [first] + own, True)
        for j in range(8):
            y_src[k, j] = acc[j]
        for j in range(7, 0, -1):
            remote(y_src.at[k, j], y_buf.at[k, j], y_send.at[k], y_recv.at[k], y_peer(j)).start()

    def wait_slots(k):
        whole = y_buf.at[k, pl.ds(1, 7)]
        remote(whole, whole, y_send.at[k], y_recv.at[k], y_peer(1)).wait_recv()
        out = [y_src[k, 0], y_buf[k, 1]]
        for j in range(2, 8):
            out[j % 2] = jnp.maximum(out[j % 2], y_buf[k, j])
        return out

    def dense(k, wait=False, total=False):
        every = [(4 * j + iota // 2).astype(jnp.float32) for j in range(8)]
        return gather_z(k, every, wait, total)

    def send_dense(k):
        for j, acc in enumerate(dense(k)):
            d_src[k, j] = acc
        for j in range(3, 0, -1):
            there = lax.rem(y + D_STEP[j], NY)
            remote(
                d_src.at[k, pl.ds(2 * there, 2)], d_buf.at[k, j], d_send.at[k], d_recv.at[k],
                d_peer(j),
            ).start()

    def send_totals():
        for j, acc in enumerate(dense(3, wait=True, total=True)):
            g_src[j] = acc
        for j in range(7, 0, -1):
            remote(g_src, g_buf.at[j], g_send, g_recv, y_peer(j)).start()

    def wait_dense(k):
        whole = d_buf.at[k, pl.ds(1, 3)]
        remote(whole, whole, d_send.at[k], d_recv.at[k], d_peer(1)).wait_recv()
        out = d_src[k, pl.ds(2 * y, 2)]
        for j in range(1, 4):
            out = jnp.maximum(out, d_buf[k, j])
        return out

    def columns_out():
        whole = f_buf.at[pl.ds(1, 7)]
        remote(whole, whole, f_send, f_recv, y_peer(1)).wait_recv()
        whole = g_buf.at[pl.ds(1, 7)]
        remote(whole, whole, g_send, g_recv, y_peer(1)).wait_recv()
        for g in range(4):
            dy = Y_STEP[2 * g][0]
            there = lax.rem(y - dy + NY, NY)
            for n in range(2):
                at = 2 * there + n
                sums = [g_src[at], g_buf[1, at]]
                for j in range(2, 8):
                    sums[j % 2] = sums[j % 2] + g_buf[j, at]
                near = scaled(f_src[n] if g == 0 else f_buf[2 * g, n], sums[0])
                far = scaled(f_buf[2 * g + 1, n], sums[1])
                low = jnp.where(half == 0, near, far)
                high = jnp.where(half == 0, far, near)
                for s in range(4):
                    at = (s % 2) * 4
                    col_out[there * 4 + n * 2 + s // 2, at : at + 2, :] = low[2 * s : 2 * s + 2, :]
                    col_out[there * 4 + n * 2 + s // 2, at + 2 : at + 4, :] = high[2 * s : 2 * s + 2, :]

    def wait_sends():
        for k in range(4):
            ref = z_buf0.at[pl.ds(1, 15)] if k == 0 else z_buf.at[k - 1, pl.ds(1, 15)]
            remote(ref, ref, z_send.at[k], z_recv.at[k, 1], z_peer(1)).wait_send()
            ref = r_buf.at[k, pl.ds(1, 7)]
            remote(ref, ref, r_send.at[k], r_recv.at[k], x_peer(1)).wait_send()
        for k in range(3):
            ref = d_buf.at[k, pl.ds(1, 3)]
            remote(ref, ref, d_send.at[k], d_recv.at[k], d_peer(1)).wait_send()
            ref = y_buf.at[k, pl.ds(1, 7)]
            remote(ref, ref, y_send.at[k], y_recv.at[k], y_peer(1)).wait_send()
        ref = meta_y.at[pl.ds(1, 7)]
        remote(ref, ref, m_send, m_recv, y_peer(1)).wait_send()
        ref = f_buf.at[pl.ds(1, 7)]
        remote(ref, ref, f_send, f_recv, y_peer(1)).wait_send()
        ref = g_buf.at[pl.ds(1, 7)]
        remote(ref, ref, g_send, g_recv, y_peer(1)).wait_send()

    scope = jax.named_scope
    one = jnp.ones((8, 128), jnp.float32)
    with scope("first_pass"):
        first_pass()
    with scope("barrier"):
        pl.semaphore_wait(barrier, len(peers))
    with scope("send_first"):
        send_rows(0)
        send_z(0)
        for j in range(7, 0, -1):
            remote(meta_src, meta_y.at[j], m_send, m_recv, y_peer(j)).start()
    with scope("wait_rows_0"):
        peak = wait_rows(0)
    with scope("column_pass_1"):
        d1 = scaled(one, peak)
        spread_rows(d1)
        column_pass(1)
    with scope("send_z_1"):
        send_z(1)
    with scope("wait_meta"):
        whole = meta_y.at[pl.ds(1, 7)]
        remote(whole, whole, m_send, m_recv, y_peer(1)).wait_recv()
    with scope("slots_0"):
        send_slots(0)
    with scope("dense_0"):
        send_dense(0)
    with scope("slots_1"):
        send_slots(1)
    with scope("wait_slots_0"):
        peaks = wait_slots(0)
    with scope("row_pass_1"):
        e1 = [scaled(one, peak) for peak in peaks]
        spread_cols(e1)
        row_pass(1)
        send_rows(1)
    with scope("dense_1"):
        send_dense(1)
    with scope("wait_slots_1"):
        peaks = wait_slots(1)
    with scope("row_pass_2"):
        e2 = [scaled(e, peak) for e, peak in zip(e1, peaks)]
        spread_cols(e2)
        row_pass(2)
        send_rows(2)
    with scope("wait_rows_1"):
        peak = wait_rows(1)
    with scope("column_pass_2"):
        d2 = scaled(d1, peak)
        spread_rows(d2)
        column_pass(2)
        send_z(2)
    with scope("wait_rows_2"):
        peak = wait_rows(2)
    with scope("column_pass_3"):
        d3 = scaled(d2, peak)
        spread_rows(d3)
        column_pass(3, total=True)
        send_z(3)
    with scope("slots_2"):
        send_slots(2)
    with scope("dense_2"):
        send_dense(2)
    with scope("totals"):
        send_totals()
    with scope("wait_dense"):
        mine = jnp.ones((2, 8, 128), jnp.float32)
        for k in range(3):
            mine = scaled(mine, wait_dense(k))
        f_src[...] = mine
        for j in range(7, 0, -1):
            remote(f_src, f_buf.at[j], f_send, f_recv, y_peer(j)).start()
    with scope("wait_slots_2"):
        peaks = wait_slots(2)
    with scope("row_pass_3"):
        e3 = [scaled(e, peak) for e, peak in zip(e2, peaks)]
        spread_cols(e3)
        row_pass(3, total=True)
        send_rows(3)
    with scope("columns_out"):
        columns_out()
    with scope("wait_rows_3"):
        row_out[...] = scaled(d3, wait_rows(3, total=True))
    with scope("wait_sends"):
        wait_sends()


def store_kernel(row_in, col_in, row_out, col_out, sem):
    copies = [
        pltpu.make_async_copy(row_in, row_out, sem.at[0]),
        pltpu.make_async_copy(col_in, col_out, sem.at[1]),
    ]
    for copy in copies:
        copy.start()
    for copy in copies:
        copy.wait()


def on_device(tiles, tile_list, tile_count):
    f32 = jnp.float32
    live = jnp.arange(SLOTS, dtype=jnp.int32)[None, :] < tile_count[:, None]
    facts = jnp.where(live, tile_list.T, -1)
    dma = pltpu.SemaphoreType.DMA
    row_scale, col_scale = pl.pallas_call(
        kernel,
        out_shape=(
            jax.ShapeDtypeStruct((8, 128), f32),
            jax.ShapeDtypeStruct((16, 8, 128), f32),
        ),
        in_specs=[
            pl.BlockSpec(memory_space=pltpu.VMEM),
            pl.BlockSpec(memory_space=pl.ANY),
        ],
        out_specs=(
            pl.BlockSpec(memory_space=pltpu.VMEM),
            pl.BlockSpec(memory_space=pltpu.VMEM),
        ),
        scratch_shapes=[
            pltpu.VMEM((SLOTS, TILE, TILE), f32),
            pltpu.VMEM((TR_DEV, TILE, 128), f32),
            pltpu.VMEM((2, 8, 128), f32),
            pltpu.VMEM((TR_DEV, TILE, 128), f32),
            pltpu.VMEM((2, 9, 128), f32),
            pltpu.VMEM((3, 2, 8, 128), f32),
            pltpu.VMEM((NZ, 9, 128), f32),
            pltpu.VMEM((3, NZ, 8, 128), f32),
            pltpu.VMEM((8, 128), f32),
            pltpu.VMEM((8, 8, 128), f32),
            pltpu.VMEM((NZ, 8, 128), f32),
            pltpu.VMEM((3, 8, 8, 128), f32),
            pltpu.VMEM((3, 8, 8, 128), f32),
            pltpu.VMEM((3, 8, 8, 128), f32),
            pltpu.VMEM((3, 4, 2, 8, 128), f32),
            pltpu.VMEM((2, 8, 128), f32),
            pltpu.VMEM((8, 2, 8, 128), f32),
            pltpu.VMEM((8, 8, 128), f32),
            pltpu.VMEM((8, 8, 8, 128), f32),
            pltpu.VMEM((4, 8, 128), f32),
            pltpu.VMEM((4, 8, 8, 128), f32),
            dma((SLOTS,)),
            dma((4,)),
            dma((4, NZ)),
            dma,
            dma,
            dma((3,)),
            dma((3,)),
            dma((3,)),
            dma((3,)),
            dma,
            dma,
            dma,
            dma,
            dma((4,)),
            dma((4,)),
        ],
        compiler_params=pltpu.CompilerParams(
            collective_id=0, has_side_effects=True, vmem_limit_bytes=52 * 1024 * 1024
        ),
    )(facts, tiles)
    row_scale, col_scale = pl.pallas_call(
        store_kernel,
        out_shape=(
            jax.ShapeDtypeStruct((8, 128), f32),
            jax.ShapeDtypeStruct((16, 8, 128), f32),
        ),
        in_specs=[pl.BlockSpec(memory_space=pltpu.VMEM)] * 2,
        out_specs=(pl.BlockSpec(memory_space=pl.ANY),) * 2,
        scratch_shapes=[dma((2,))],
    )(row_scale, col_scale)
    return row_scale.reshape(-1), col_scale.reshape(-1)


def solution(mesh):
    return jax.shard_map(
        on_device,
        mesh=mesh,
        in_specs=(P(("row", "col"), None, None), P(("row", "col"), None), P(("row", "col"))),
        out_specs=(P("row"), P("col")),
        check_vma=False,
    )
```

```python
import functools

import jax
import jax.numpy as jnp
from jax import lax
from jax.experimental import pallas as pl
from jax.experimental.pallas import tpu as pltpu
from jax.sharding import PartitionSpec as P

MESH = pl.DeviceIdType.MESH
TR_DEV = 2
TC_DEV = 32
SLOTS = 4
TILE = 512
EPS = 1e-06
NY, NZ, NX, NC = 4, 16, 4, 2

Z_STEP = [0] + [(q + 1) // 2 if q % 2 else -(q // 2) for q in range(1, NZ)]
Y_STEP = [(dy, p) for dy in (0, 1, 3, 2) for p in (0, 1)]
X_STEP = [(dx, dc) for dx in (0, 1, 3, 2) for dc in (0, 1)]
D_STEP = [0, 1, 3, 2]


def scaled(value, peak):
    return value / jnp.sqrt(value * peak + EPS)


def kernel(
    facts_ref, tiles_ref, row_out, col_out,
    tile, by_row, by_col, fold, z_src0, z_src, z_buf0, z_buf, meta_src, meta_y, meta_z,
    y_src, y_buf, d_src, d_buf, f_src, f_buf, g_src, g_buf, r_src, r_buf,
    load_sem, z_send, z_recv, m_send, m_recv, y_send, y_recv, d_send, d_recv,
    f_send, f_recv, g_send, g_recv, r_send, r_recv,
):
    row, col = lax.axis_index("row"), lax.axis_index("col")
    y, z = row // NZ, lax.rem(row, NZ)
    x, core = col // NC, lax.rem(col, NC)
    half = lax.rem(z, 2)

    def z_peer(q):
        return (y * NZ + lax.rem(z + Z_STEP[q] + NZ, NZ), col)

    def y_peer(j):
        dy, p = Y_STEP[j]
        return (lax.rem(y + dy, NY) * NZ + (z + 1 - 2 * half if p else z), col)

    def x_peer(j):
        dx, dc = X_STEP[j]
        return (row, lax.rem(x + dx, NX) * NC + lax.rem(core + dc, NC))

    def d_peer(j):
        return (lax.rem(y + D_STEP[j], NY) * NZ + z, col)

    def remote(src, dst, send, recv, peer):
        return pltpu.make_async_remote_copy(
            src_ref=src, dst_ref=dst, send_sem=send, recv_sem=recv,
            device_id=peer, device_id_type=MESH,
        )

    barrier = pltpu.get_barrier_semaphore()
    peers = [z_peer(q) for q in range(NZ - 1, 0, -1)]
    peers += [y_peer(j) for j in range(7, 1, -1)]
    peers += [x_peer(j) for j in range(7, 0, -1)]
    for peer in peers:
        pl.semaphore_signal(barrier, inc=1, device_id=peer, device_id_type=MESH)

    loads = [
        pltpu.make_async_copy(tiles_ref.at[s], tile.at[s], load_sem.at[s]) for s in range(SLOTS)
    ]
    for load in loads:
        load.start()

    iota = lax.broadcasted_iota(jnp.int32, (8, 128), 0)
    lane = lax.broadcasted_iota(jnp.int32, (8, 128), 1)

    def wide(value):
        return jnp.broadcast_to(value, (8, 128))

    def tall(value, rows):
        return jnp.broadcast_to(value[None], (rows // 8, 8, 128)).reshape(rows, 128)

    second, in_row = [], []
    meta = jnp.full((8, 128), -1.0, jnp.float32)
    meta_line = jnp.full((1, 128), -1.0, jnp.float32)
    for s in range(SLOTS):
        tile_row = wide(facts_ref[0:1, s : s + 1])
        live = tile_row >= 0
        tile_row = tile_row - row * TR_DEV
        second.append(jnp.where(tile_row > 0, 1.0, 0.0))
        in_row.append(
            [jnp.where(live, jnp.where(tile_row == t, 1.0, 0.0), 0.0) for t in range(TR_DEV)]
        )
        at = jnp.where(live, wide(facts_ref[1:2, s : s + 1]) - col * TC_DEV, -1)
        at = at.astype(jnp.float32)
        meta = jnp.where(iota // 2 == s, at, meta)
        meta_line = jnp.where(lane[0:1] // 2 == s, at[0:1], meta_line)
    meta_src[...] = meta
    for p in range(2):
        z_src0[p, 8:9, :] = meta_line

    def combine(total):
        return (jnp.add, jnp.sum) if total else (jnp.maximum, jnp.max)

    def put_columns(k, s, acc, fold_of):
        for b in range(4):
            line = fold_of(acc[b], axis=0, keepdims=True)
            at = 2 * s + b % 2
            which = half if b // 2 == 0 else 1 - half
            if k == 0:
                z_src0[which, at : at + 1, :] = line
            else:
                z_src[k - 1, which, at : at + 1, :] = line

    def put_rows(k, fold_of):
        res = jnp.zeros((8, 128), jnp.float32)
        for t in range(TR_DEV):
            for blk in range(4):
                line = fold_of(fold[t, blk * 128 : (blk + 1) * 128, :].T, axis=0, keepdims=True)
                res = jnp.where(iota == t * 4 + blk, line, res)
        r_src[k] = res

    zeros = (jnp.zeros((8, 128), jnp.float32),) * 4

    def first_pass():
        for s in range(SLOTS):
            loads[s].wait()

            def body(c, acc):
                start = pl.multiple_of(c * 32, 32)
                acc, part = list(acc), None
                for b in range(4):
                    piece = jnp.abs(tile[s, pl.ds(start, 32), b * 128 : (b + 1) * 128])
                    tile[s, pl.ds(start, 32), b * 128 : (b + 1) * 128] = piece
                    acc[b] = jnp.maximum(acc[b], jnp.max(piece.reshape(4, 8, 128), axis=0))
                    part = piece if part is None else jnp.maximum(part, piece)
                for t in range(TR_DEV):
                    side = jnp.where(tall(in_row[s][t], 32) > 0.5, part, 0.0)
                    if s:
                        side = jnp.maximum(side, fold[t, pl.ds(start, 32), :])
                    fold[t, pl.ds(start, 32), :] = side
                return tuple(acc)

            put_columns(0, s, lax.fori_loop(0, TILE // 32, body, zeros, unroll=2), jnp.max)
        put_rows(0, jnp.max)

    def column_pass(k, total=False):
        join, fold_of = combine(total)
        accs = []
        for s in range(SLOTS):

            def body(c, acc):
                start = pl.multiple_of(c * 64, 64)
                weight = jnp.where(
                    tall(second[s], 64) > 0.5,
                    by_row[1, pl.ds(start, 64), :],
                    by_row[0, pl.ds(start, 64), :],
                )
                acc = list(acc)
                for b in range(4):
                    part = tile[s, pl.ds(start, 64), b * 128 : (b + 1) * 128] * weight
                    acc[b] = join(acc[b], fold_of(part.reshape(8, 8, 128), axis=0))
                return tuple(acc)

            accs.append(lax.fori_loop(0, TILE // 64, body, zeros, unroll=4))
        for s in range(SLOTS):
            put_columns(k, s, accs[s], fold_of)

    def row_pass(k, total=False):
        join, fold_of = combine(total)

        def body(c, carry):
            start = pl.multiple_of(c * 32, 32)
            sides = [jnp.zeros((32, 128), jnp.float32)] * TR_DEV
            for s in range(SLOTS):
                part = None
                for b in range(4):
                    at = 2 * s + b % 2
                    piece = tile[s, pl.ds(start, 32), b * 128 : (b + 1) * 128]
                    piece = piece * by_col[b // 2, at : at + 1, :]
                    part = piece if part is None else join(part, piece)
                sides = [
                    join(side, jnp.where(tall(in_row[s][t], 32) > 0.5, part, 0.0))
                    for t, side in enumerate(sides)
                ]
            for t in range(TR_DEV):
                fold[t, pl.ds(start, 32), :] = sides[t]
            return carry

        lax.fori_loop(0, TILE // 32, body, 0, unroll=2)
        put_rows(k, fold_of)

    def send_rows(k):
        for j in range(7, 0, -1):
            remote(r_src.at[k], r_buf.at[k, j], r_send.at[k], r_recv.at[k], x_peer(j)).start()

    def wait_rows(k, total=False):
        join, _ = combine(total)
        whole = r_buf.at[k, pl.ds(1, 7)]
        remote(whole, whole, r_send.at[k], r_recv.at[k], x_peer(1)).wait_recv()
        out = r_src[k]
        for j in range(1, 8):
            out = join(out, r_buf[k, j])
        return out

    def spread_rows(d):
        for t in range(TR_DEV):
            for blk in range(4):
                at = t * 4 + blk
                wide = jnp.broadcast_to(d[at : at + 1, :], (128, 128))
                by_row[t, blk * 128 : (blk + 1) * 128, :] = wide.T

    def spread_cols(e):
        for p in range(2):
            by_col[half if p == 0 else 1 - half] = e[p]

    def z_refs(k, q):
        if k == 0:
            return z_buf0.at[q]
        return z_buf.at[k - 1, q]

    def z_from(k, p):
        return z_src0.at[p] if k == 0 else z_src.at[k - 1, p]

    def send_z(k):
        for q in range(NZ - 1, 0, -1):
            remote(
                z_from(k, Z_STEP[q] % 2), z_refs(k, q), z_send.at[k], z_recv.at[k, q], z_peer(q)
            ).start()

    def gather_z(k, targets, wait, total=False):
        join, _ = combine(total)

        def add(acc, value, at):
            acc = list(acc)
            for turn in range(4):
                v = pltpu.roll(value, 2 * turn, 0) if turn else value
                m = pltpu.roll(at, 2 * turn, 0) if turn else at
                for j in range(8):
                    acc[j] = join(acc[j], jnp.where(m == targets[j], v, 0.0))
            return tuple(acc)

        def body(q, acc):
            if wait:
                ref = z_refs(k, q)
                remote(ref, ref, z_send.at[k], z_recv.at[k, q], z_peer(1)).wait_recv()
            value = z_buf0[q, 0:8, :] if k == 0 else z_buf[k - 1, q]
            if k == 0 and wait:
                line = jnp.where(lane == iota, z_buf0[q, 8:9, :], -1.0)
                at = jnp.broadcast_to(jnp.max(line, axis=1, keepdims=True), (8, 128))
                meta_z[q] = at
            else:
                at = meta_z[q]
            return add(acc, value, at)

        own = z_src0[0, 0:8, :] if k == 0 else z_src[k - 1, 0]
        acc = add((jnp.zeros((8, 128), jnp.float32),) * 8, own, meta_src[...])
        return lax.fori_loop(1, NZ, body, acc)

    def send_slots(k):
        own = []
        for j in range(1, 8):
            dy, p = Y_STEP[j]
            at = meta_y[Y_STEP.index(((NY - dy) % NY, p))]
            own.append(jnp.where(at < 0, -2.0, at))
        first = jnp.where(meta_src[...] < 0, -2.0, meta_src[...])
        acc = gather_z(k, [first] + own, True)
        for j in range(8):
            y_src[k, j] = acc[j]
        for j in range(7, 0, -1):
            remote(y_src.at[k, j], y_buf.at[k, j], y_send.at[k], y_recv.at[k], y_peer(j)).start()

    def wait_slots(k):
        whole = y_buf.at[k, pl.ds(1, 7)]
        remote(whole, whole, y_send.at[k], y_recv.at[k], y_peer(1)).wait_recv()
        out = [y_src[k, 0], y_buf[k, 1]]
        for j in range(2, 8):
            out[j % 2] = jnp.maximum(out[j % 2], y_buf[k, j])
        return out

    def dense(k, wait=False, total=False):
        every = [(4 * j + iota // 2).astype(jnp.float32) for j in range(8)]
        return gather_z(k, every, wait, total)

    def send_dense(k):
        for j, acc in enumerate(dense(k)):
            d_src[k, j] = acc
        for j in range(3, 0, -1):
            there = lax.rem(y + D_STEP[j], NY)
            remote(
                d_src.at[k, pl.ds(2 * there, 2)], d_buf.at[k, j], d_send.at[k], d_recv.at[k],
                d_peer(j),
            ).start()

    def send_totals():
        for j, acc in enumerate(dense(3, wait=True, total=True)):
            g_src[j] = acc
        for j in range(7, 0, -1):
            remote(g_src, g_buf.at[j], g_send, g_recv, y_peer(j)).start()

    def wait_dense(k):
        whole = d_buf.at[k, pl.ds(1, 3)]
        remote(whole, whole, d_send.at[k], d_recv.at[k], d_peer(1)).wait_recv()
        out = d_src[k, pl.ds(2 * y, 2)]
        for j in range(1, 4):
            out = jnp.maximum(out, d_buf[k, j])
        return out

    def columns_out():
        whole = f_buf.at[pl.ds(1, 7)]
        remote(whole, whole, f_send, f_recv, y_peer(1)).wait_recv()
        whole = g_buf.at[pl.ds(1, 7)]
        remote(whole, whole, g_send, g_recv, y_peer(1)).wait_recv()
        for g in range(4):
            dy = Y_STEP[2 * g][0]
            there = lax.rem(y - dy + NY, NY)
            for n in range(2):
                at = 2 * there + n
                sums = [g_src[at], g_buf[1, at]]
                for j in range(2, 8):
                    sums[j % 2] = sums[j % 2] + g_buf[j, at]
                near = scaled(f_src[n] if g == 0 else f_buf[2 * g, n], sums[0])
                far = scaled(f_buf[2 * g + 1, n], sums[1])
                low = jnp.where(half == 0, near, far)
                high = jnp.where(half == 0, far, near)
                for s in range(4):
                    at = (s % 2) * 4
                    col_out[there * 4 + n * 2 + s // 2, at : at + 2, :] = low[2 * s : 2 * s + 2, :]
                    col_out[there * 4 + n * 2 + s // 2, at + 2 : at + 4, :] = high[2 * s : 2 * s + 2, :]

    def wait_sends():
        for k in range(4):
            ref = z_buf0.at[pl.ds(1, 15)] if k == 0 else z_buf.at[k - 1, pl.ds(1, 15)]
            remote(ref, ref, z_send.at[k], z_recv.at[k, 1], z_peer(1)).wait_send()
            ref = r_buf.at[k, pl.ds(1, 7)]
            remote(ref, ref, r_send.at[k], r_recv.at[k], x_peer(1)).wait_send()
        for k in range(3):
            ref = d_buf.at[k, pl.ds(1, 3)]
            remote(ref, ref, d_send.at[k], d_recv.at[k], d_peer(1)).wait_send()
            ref = y_buf.at[k, pl.ds(1, 7)]
            remote(ref, ref, y_send.at[k], y_recv.at[k], y_peer(1)).wait_send()
        ref = meta_y.at[pl.ds(1, 7)]
        remote(ref, ref, m_send, m_recv, y_peer(1)).wait_send()
        ref = f_buf.at[pl.ds(1, 7)]
        remote(ref, ref, f_send, f_recv, y_peer(1)).wait_send()
        ref = g_buf.at[pl.ds(1, 7)]
        remote(ref, ref, g_send, g_recv, y_peer(1)).wait_send()

    one = jnp.ones((8, 128), jnp.float32)
    first_pass()
    pl.semaphore_wait(barrier, len(peers))
    send_rows(0)
    send_z(0)
    for j in range(7, 0, -1):
        remote(meta_src, meta_y.at[j], m_send, m_recv, y_peer(j)).start()
    peak = wait_rows(0)
    d1 = scaled(one, peak)
    spread_rows(d1)
    column_pass(1)
    send_z(1)
    whole = meta_y.at[pl.ds(1, 7)]
    remote(whole, whole, m_send, m_recv, y_peer(1)).wait_recv()
    send_slots(0)
    send_dense(0)
    send_slots(1)
    peaks = wait_slots(0)
    e1 = [scaled(one, peak) for peak in peaks]
    spread_cols(e1)
    row_pass(1)
    send_rows(1)
    send_dense(1)
    peaks = wait_slots(1)
    e2 = [scaled(e, peak) for e, peak in zip(e1, peaks)]
    spread_cols(e2)
    row_pass(2)
    send_rows(2)
    peak = wait_rows(1)
    d2 = scaled(d1, peak)
    spread_rows(d2)
    column_pass(2)
    send_z(2)
    peak = wait_rows(2)
    d3 = scaled(d2, peak)
    spread_rows(d3)
    column_pass(3, total=True)
    send_z(3)
    send_slots(2)
    send_dense(2)
    send_totals()
    mine = jnp.ones((2, 8, 128), jnp.float32)
    for k in range(3):
        mine = scaled(mine, wait_dense(k))
    f_src[...] = mine
    for j in range(7, 0, -1):
        remote(f_src, f_buf.at[j], f_send, f_recv, y_peer(j)).start()
    peaks = wait_slots(2)
    e3 = [scaled(e, peak) for e, peak in zip(e2, peaks)]
    spread_cols(e3)
    row_pass(3, total=True)
    send_rows(3)
    columns_out()
    row_out[...] = scaled(d3, wait_rows(3, total=True))
    wait_sends()

def on_device(tiles, tile_list, tile_count):
    f32 = jnp.float32
    live = jnp.arange(SLOTS, dtype=jnp.int32)[None, :] < tile_count[:, None]
    facts = jnp.where(live, tile_list.T, -1)
    dma = pltpu.SemaphoreType.DMA
    row_scale, col_scale = pl.pallas_call(
        kernel,
        out_shape=(
            jax.ShapeDtypeStruct((8, 128), f32),
            jax.ShapeDtypeStruct((16, 8, 128), f32),
        ),
        in_specs=[
            pl.BlockSpec(memory_space=pltpu.VMEM),
            pl.BlockSpec(memory_space=pl.ANY),
        ],
        out_specs=(
            pl.BlockSpec(memory_space=pltpu.VMEM),
            pl.BlockSpec(memory_space=pltpu.VMEM),
        ),
        scratch_shapes=[
            pltpu.VMEM((SLOTS, TILE, TILE), f32),
            pltpu.VMEM((TR_DEV, TILE, 128), f32),
            pltpu.VMEM((2, 8, 128), f32),
            pltpu.VMEM((TR_DEV, TILE, 128), f32),
            pltpu.VMEM((2, 9, 128), f32),
            pltpu.VMEM((3, 2, 8, 128), f32),
            pltpu.VMEM((NZ, 9, 128), f32),
            pltpu.VMEM((3, NZ, 8, 128), f32),
            pltpu.VMEM((8, 128), f32),
            pltpu.VMEM((8, 8, 128), f32),
            pltpu.VMEM((NZ, 8, 128), f32),
            pltpu.VMEM((3, 8, 8, 128), f32),
            pltpu.VMEM((3, 8, 8, 128), f32),
            pltpu.VMEM((3, 8, 8, 128), f32),
            pltpu.VMEM((3, 4, 2, 8, 128), f32),
            pltpu.VMEM((2, 8, 128), f32),
            pltpu.VMEM((8, 2, 8, 128), f32),
            pltpu.VMEM((8, 8, 128), f32),
            pltpu.VMEM((8, 8, 8, 128), f32),
            pltpu.VMEM((4, 8, 128), f32),
            pltpu.VMEM((4, 8, 8, 128), f32),
            dma((SLOTS,)),
            dma((4,)),
            dma((4, NZ)),
            dma,
            dma,
            dma((3,)),
            dma((3,)),
            dma((3,)),
            dma((3,)),
            dma,
            dma,
            dma,
            dma,
            dma((4,)),
            dma((4,)),
        ],
        compiler_params=pltpu.CompilerParams(
            collective_id=0, has_side_effects=True, vmem_limit_bytes=52 * 1024 * 1024
        ),
    )(facts, tiles)
    return row_scale.reshape(-1), col_scale.reshape(-1)


def solution(mesh):
    return jax.shard_map(
        on_device,
        mesh=mesh,
        in_specs=(P(("row", "col"), None, None), P(("row", "col"), None), P(("row", "col"))),
        out_specs=(P("row"), P("col")),
        check_vma=False,
    )
```

```python
import functools

import jax
import jax.numpy as jnp
from jax import lax
from jax.experimental import pallas as pl
from jax.experimental.pallas import tpu as pltpu
from jax.sharding import PartitionSpec as P

MESH = pl.DeviceIdType.MESH
TR_DEV = 2
TC_DEV = 32
SLOTS = 4
TILE = 512
EPS = 1e-06
NY, NZ, NX, NC = 4, 16, 4, 2

Z_STEP = [0] + [(q + 1) // 2 if q % 2 else -(q // 2) for q in range(1, NZ)]
Y_STEP = [(dy, p) for dy in (0, 1, 3, 2) for p in (0, 1)]
X_STEP = [(dx, dc) for dx in (0, 1, 3, 2) for dc in (0, 1)]
D_STEP = [0, 1, 3, 2]


def scaled(value, peak):
    return value / jnp.sqrt(value * peak + EPS)


def kernel(
    facts_ref, tiles_ref, row_out, col_out,
    tile, by_row, by_col, fold, z_src0, z_src, z_buf0, z_buf, meta_src, meta_y, meta_z,
    y_src, y_buf, d_src, d_buf, f_src, f_buf, g_src, g_buf, r_src, r_buf,
    load_sem, z_send, z_recv, m_send, m_recv, y_send, y_recv, d_send, d_recv,
    f_send, f_recv, g_send, g_recv, r_send, r_recv, far_sem,
):
    row, col = lax.axis_index("row"), lax.axis_index("col")
    y, z = row // NZ, lax.rem(row, NZ)
    x, core = col // NC, lax.rem(col, NC)
    half = lax.rem(z, 2)

    def z_peer(q):
        return (y * NZ + lax.rem(z + Z_STEP[q] + NZ, NZ), col)

    def y_peer(j):
        dy, p = Y_STEP[j]
        return (lax.rem(y + dy, NY) * NZ + (z + 1 - 2 * half if p else z), col)

    def x_peer(j):
        dx, dc = X_STEP[j]
        return (row, lax.rem(x + dx, NX) * NC + lax.rem(core + dc, NC))

    def d_peer(j):
        return (lax.rem(y + D_STEP[j], NY) * NZ + z, col)

    def remote(src, dst, send, recv, peer):
        return pltpu.make_async_remote_copy(
            src_ref=src, dst_ref=dst, send_sem=send, recv_sem=recv,
            device_id=peer, device_id_type=MESH,
        )

    barrier = pltpu.get_barrier_semaphore()
    peers = [z_peer(q) for q in range(8, 0, -1)]
    peers += [y_peer(j) for j in range(7, 1, -1)]
    peers += [x_peer(j) for j in range(7, 0, -1)]
    for peer in peers:
        pl.semaphore_signal(barrier, inc=1, device_id=peer, device_id_type=MESH)

    loads = [
        pltpu.make_async_copy(tiles_ref.at[s], tile.at[s], load_sem.at[s]) for s in range(SLOTS)
    ]
    for load in loads:
        load.start()

    iota = lax.broadcasted_iota(jnp.int32, (8, 128), 0)
    lane = lax.broadcasted_iota(jnp.int32, (8, 128), 1)

    def wide(value):
        return jnp.broadcast_to(value, (8, 128))

    def tall(value, rows):
        return jnp.broadcast_to(value[None], (rows // 8, 8, 128)).reshape(rows, 128)

    second, in_row = [], []
    meta = jnp.full((8, 128), -1.0, jnp.float32)
    meta_line = jnp.full((1, 128), -1.0, jnp.float32)
    for s in range(SLOTS):
        tile_row = wide(facts_ref[0:1, s : s + 1])
        live = tile_row >= 0
        tile_row = tile_row - row * TR_DEV
        second.append(jnp.where(tile_row > 0, 1.0, 0.0))
        in_row.append(
            [jnp.where(live, jnp.where(tile_row == t, 1.0, 0.0), 0.0) for t in range(TR_DEV)]
        )
        at = jnp.where(live, wide(facts_ref[1:2, s : s + 1]) - col * TC_DEV, -1)
        at = at.astype(jnp.float32)
        meta = jnp.where(iota // 2 == s, at, meta)
        meta_line = jnp.where(lane[0:1] // 2 == s, at[0:1], meta_line)
    meta_src[...] = meta
    for p in range(2):
        z_src0[p, 8:9, :] = meta_line

    def combine(total):
        return (jnp.add, jnp.sum) if total else (jnp.maximum, jnp.max)

    def put_columns(k, s, acc, fold_of):
        for b in range(4):
            line = fold_of(acc[b], axis=0, keepdims=True)
            at = 2 * s + b % 2
            which = half if b // 2 == 0 else 1 - half
            if k == 0:
                z_src0[which, at : at + 1, :] = line
            else:
                z_src[k - 1, which, at : at + 1, :] = line

    def put_rows(k, fold_of):
        res = jnp.zeros((8, 128), jnp.float32)
        for t in range(TR_DEV):
            for blk in range(4):
                line = fold_of(fold[t, blk * 128 : (blk + 1) * 128, :].T, axis=0, keepdims=True)
                res = jnp.where(iota == t * 4 + blk, line, res)
        r_src[k] = res

    zeros = (jnp.zeros((8, 128), jnp.float32),) * 4

    def first_pass():
        for s in range(SLOTS):
            loads[s].wait()

            def body(c, acc):
                start = pl.multiple_of(c * 32, 32)
                acc, part = list(acc), None
                for b in range(4):
                    piece = jnp.abs(tile[s, pl.ds(start, 32), b * 128 : (b + 1) * 128])
                    tile[s, pl.ds(start, 32), b * 128 : (b + 1) * 128] = piece
                    acc[b] = jnp.maximum(acc[b], jnp.max(piece.reshape(4, 8, 128), axis=0))
                    part = piece if part is None else jnp.maximum(part, piece)
                for t in range(TR_DEV):
                    side = jnp.where(tall(in_row[s][t], 32) > 0.5, part, 0.0)
                    if s:
                        side = jnp.maximum(side, fold[t, pl.ds(start, 32), :])
                    fold[t, pl.ds(start, 32), :] = side
                return tuple(acc)

            put_columns(0, s, lax.fori_loop(0, TILE // 32, body, zeros, unroll=2), jnp.max)
        put_rows(0, jnp.max)

    def column_pass(k, total=False):
        join, fold_of = combine(total)
        accs = []
        for s in range(SLOTS):

            def body(c, acc):
                start = pl.multiple_of(c * 64, 64)
                weight = jnp.where(
                    tall(second[s], 64) > 0.5,
                    by_row[1, pl.ds(start, 64), :],
                    by_row[0, pl.ds(start, 64), :],
                )
                acc = list(acc)
                for b in range(4):
                    part = tile[s, pl.ds(start, 64), b * 128 : (b + 1) * 128] * weight
                    acc[b] = join(acc[b], fold_of(part.reshape(8, 8, 128), axis=0))
                return tuple(acc)

            accs.append(lax.fori_loop(0, TILE // 64, body, zeros, unroll=4))
        for s in range(SLOTS):
            put_columns(k, s, accs[s], fold_of)

    def row_pass(k, total=False):
        join, fold_of = combine(total)

        def body(c, carry):
            start = pl.multiple_of(c * 32, 32)
            sides = [jnp.zeros((32, 128), jnp.float32)] * TR_DEV
            for s in range(SLOTS):
                part = None
                for b in range(4):
                    at = 2 * s + b % 2
                    piece = tile[s, pl.ds(start, 32), b * 128 : (b + 1) * 128]
                    piece = piece * by_col[b // 2, at : at + 1, :]
                    part = piece if part is None else join(part, piece)
                sides = [
                    join(side, jnp.where(tall(in_row[s][t], 32) > 0.5, part, 0.0))
                    for t, side in enumerate(sides)
                ]
            for t in range(TR_DEV):
                fold[t, pl.ds(start, 32), :] = sides[t]
            return carry

        lax.fori_loop(0, TILE // 32, body, 0, unroll=2)
        put_rows(k, fold_of)

    def send_rows(k):
        for j in range(7, 0, -1):
            remote(r_src.at[k], r_buf.at[k, j], r_send.at[k], r_recv.at[k], x_peer(j)).start()

    def wait_rows(k, total=False):
        join, _ = combine(total)
        whole = r_buf.at[k, pl.ds(1, 7)]
        remote(whole, whole, r_send.at[k], r_recv.at[k], x_peer(1)).wait_recv()
        out = r_src[k]
        for j in range(1, 8):
            out = join(out, r_buf[k, j])
        return out

    def spread_rows(d):
        for t in range(TR_DEV):
            for blk in range(4):
                at = t * 4 + blk
                wide = jnp.broadcast_to(d[at : at + 1, :], (128, 128))
                by_row[t, blk * 128 : (blk + 1) * 128, :] = wide.T

    def spread_cols(e):
        for p in range(2):
            by_col[half if p == 0 else 1 - half] = e[p]

    def z_refs(k, q):
        if k == 0:
            return z_buf0.at[q]
        return z_buf.at[k - 1, q]

    def z_from(k, p):
        return z_src0.at[p] if k == 0 else z_src.at[k - 1, p]

    def send_z(k):
        for q in range(NZ - 1, 0, -1):
            remote(
                z_from(k, Z_STEP[q] % 2), z_refs(k, q), z_send.at[k], z_recv.at[k, q], z_peer(q)
            ).start()

    def gather_z(k, targets, wait, total=False):
        join, _ = combine(total)

        def add(acc, value, at):
            acc = list(acc)
            for turn in range(4):
                v = pltpu.roll(value, 2 * turn, 0) if turn else value
                m = pltpu.roll(at, 2 * turn, 0) if turn else at
                for j in range(8):
                    acc[j] = join(acc[j], jnp.where(m == targets[j], v, 0.0))
            return tuple(acc)

        def body(q, acc):
            if wait:
                ref = z_refs(k, q)
                remote(ref, ref, z_send.at[k], z_recv.at[k, q], z_peer(1)).wait_recv()
            value = z_buf0[q, 0:8, :] if k == 0 else z_buf[k - 1, q]
            if k == 0 and wait:
                line = jnp.where(lane == iota, z_buf0[q, 8:9, :], -1.0)
                at = jnp.broadcast_to(jnp.max(line, axis=1, keepdims=True), (8, 128))
                meta_z[q] = at
            else:
                at = meta_z[q]
            return add(acc, value, at)

        own = z_src0[0, 0:8, :] if k == 0 else z_src[k - 1, 0]
        acc = add((jnp.zeros((8, 128), jnp.float32),) * 8, own, meta_src[...])
        return lax.fori_loop(1, NZ, body, acc)

    def send_slots(k):
        own = []
        for j in range(1, 8):
            dy, p = Y_STEP[j]
            at = meta_y[Y_STEP.index(((NY - dy) % NY, p))]
            own.append(jnp.where(at < 0, -2.0, at))
        first = jnp.where(meta_src[...] < 0, -2.0, meta_src[...])
        acc = gather_z(k, [first] + own, True)
        for j in range(8):
            y_src[k, j] = acc[j]
        for j in range(7, 0, -1):
            remote(y_src.at[k, j], y_buf.at[k, j], y_send.at[k], y_recv.at[k], y_peer(j)).start()

    def wait_slots(k):
        whole = y_buf.at[k, pl.ds(1, 7)]
        remote(whole, whole, y_send.at[k], y_recv.at[k], y_peer(1)).wait_recv()
        out = [y_src[k, 0], y_buf[k, 1]]
        for j in range(2, 8):
            out[j % 2] = jnp.maximum(out[j % 2], y_buf[k, j])
        return out

    def dense(k, wait=False, total=False):
        every = [(4 * j + iota // 2).astype(jnp.float32) for j in range(8)]
        return gather_z(k, every, wait, total)

    def send_dense(k):
        for j, acc in enumerate(dense(k)):
            d_src[k, j] = acc
        for j in range(3, 0, -1):
            there = lax.rem(y + D_STEP[j], NY)
            remote(
                d_src.at[k, pl.ds(2 * there, 2)], d_buf.at[k, j], d_send.at[k], d_recv.at[k],
                d_peer(j),
            ).start()

    def send_totals():
        for j, acc in enumerate(dense(3, wait=True, total=True)):
            g_src[j] = acc
        for j in range(7, 0, -1):
            remote(g_src, g_buf.at[j], g_send, g_recv, y_peer(j)).start()

    def wait_dense(k):
        whole = d_buf.at[k, pl.ds(1, 3)]
        remote(whole, whole, d_send.at[k], d_recv.at[k], d_peer(1)).wait_recv()
        out = d_src[k, pl.ds(2 * y, 2)]
        for j in range(1, 4):
            out = jnp.maximum(out, d_buf[k, j])
        return out

    def columns_out():
        whole = f_buf.at[pl.ds(1, 7)]
        remote(whole, whole, f_send, f_recv, y_peer(1)).wait_recv()
        whole = g_buf.at[pl.ds(1, 7)]
        remote(whole, whole, g_send, g_recv, y_peer(1)).wait_recv()
        for g in range(4):
            dy = Y_STEP[2 * g][0]
            there = lax.rem(y - dy + NY, NY)
            for n in range(2):
                at = 2 * there + n
                sums = [g_src[at], g_buf[1, at]]
                for j in range(2, 8):
                    sums[j % 2] = sums[j % 2] + g_buf[j, at]
                near = scaled(f_src[n] if g == 0 else f_buf[2 * g, n], sums[0])
                far = scaled(f_buf[2 * g + 1, n], sums[1])
                low = jnp.where(half == 0, near, far)
                high = jnp.where(half == 0, far, near)
                for s in range(4):
                    at = (s % 2) * 4
                    col_out[there * 4 + n * 2 + s // 2, at : at + 2, :] = low[2 * s : 2 * s + 2, :]
                    col_out[there * 4 + n * 2 + s // 2, at + 2 : at + 4, :] = high[2 * s : 2 * s + 2, :]

    def wait_sends():
        for k in range(4):
            ref = z_buf0.at[pl.ds(1, 15)] if k == 0 else z_buf.at[k - 1, pl.ds(1, 15)]
            remote(ref, ref, z_send.at[k], z_recv.at[k, 1], z_peer(1)).wait_send()
            ref = r_buf.at[k, pl.ds(1, 7)]
            remote(ref, ref, r_send.at[k], r_recv.at[k], x_peer(1)).wait_send()
        for k in range(3):
            ref = d_buf.at[k, pl.ds(1, 3)]
            remote(ref, ref, d_send.at[k], d_recv.at[k], d_peer(1)).wait_send()
            ref = y_buf.at[k, pl.ds(1, 7)]
            remote(ref, ref, y_send.at[k], y_recv.at[k], y_peer(1)).wait_send()
        ref = meta_y.at[pl.ds(1, 7)]
        remote(ref, ref, m_send, m_recv, y_peer(1)).wait_send()
        ref = f_buf.at[pl.ds(1, 7)]
        remote(ref, ref, f_send, f_recv, y_peer(1)).wait_send()
        ref = g_buf.at[pl.ds(1, 7)]
        remote(ref, ref, g_send, g_recv, y_peer(1)).wait_send()

    one = jnp.ones((8, 128), jnp.float32)
    first_pass()
    pl.semaphore_wait(barrier, len(peers))
    for q in (7, 8):
        pl.semaphore_signal(far_sem, inc=1, device_id=z_peer(q), device_id_type=MESH)
    send_rows(0)
    pl.semaphore_wait(far_sem, 2)
    send_z(0)
    for j in range(7, 0, -1):
        remote(meta_src, meta_y.at[j], m_send, m_recv, y_peer(j)).start()
    peak = wait_rows(0)
    d1 = scaled(one, peak)
    spread_rows(d1)
    column_pass(1)
    send_z(1)
    whole = meta_y.at[pl.ds(1, 7)]
    remote(whole, whole, m_send, m_recv, y_peer(1)).wait_recv()
    send_slots(0)
    send_dense(0)
    send_slots(1)
    peaks = wait_slots(0)
    e1 = [scaled(one, peak) for peak in peaks]
    spread_cols(e1)
    row_pass(1)
    send_rows(1)
    send_dense(1)
    peaks = wait_slots(1)
    e2 = [scaled(e, peak) for e, peak in zip(e1, peaks)]
    spread_cols(e2)
    row_pass(2)
    send_rows(2)
    peak = wait_rows(1)
    d2 = scaled(d1, peak)
    spread_rows(d2)
    column_pass(2)
    send_z(2)
    peak = wait_rows(2)
    d3 = scaled(d2, peak)
    spread_rows(d3)
    column_pass(3, total=True)
    send_z(3)
    send_slots(2)
    send_dense(2)
    send_totals()
    mine = jnp.ones((2, 8, 128), jnp.float32)
    for k in range(3):
        mine = scaled(mine, wait_dense(k))
    f_src[...] = mine
    for j in range(7, 0, -1):
        remote(f_src, f_buf.at[j], f_send, f_recv, y_peer(j)).start()
    peaks = wait_slots(2)
    e3 = [scaled(e, peak) for e, peak in zip(e2, peaks)]
    spread_cols(e3)
    row_pass(3, total=True)
    send_rows(3)
    columns_out()
    row_out[...] = scaled(d3, wait_rows(3, total=True))
    wait_sends()

def on_device(tiles, tile_list, tile_count):
    f32 = jnp.float32
    live = jnp.arange(SLOTS, dtype=jnp.int32)[None, :] < tile_count[:, None]
    facts = jnp.where(live, tile_list.T, -1)
    dma = pltpu.SemaphoreType.DMA
    row_scale, col_scale = pl.pallas_call(
        kernel,
        out_shape=(
            jax.ShapeDtypeStruct((8, 128), f32),
            jax.ShapeDtypeStruct((16, 8, 128), f32),
        ),
        in_specs=[
            pl.BlockSpec(memory_space=pltpu.VMEM),
            pl.BlockSpec(memory_space=pl.ANY),
        ],
        out_specs=(
            pl.BlockSpec(memory_space=pltpu.VMEM),
            pl.BlockSpec(memory_space=pltpu.VMEM),
        ),
        scratch_shapes=[
            pltpu.VMEM((SLOTS, TILE, TILE), f32),
            pltpu.VMEM((TR_DEV, TILE, 128), f32),
            pltpu.VMEM((2, 8, 128), f32),
            pltpu.VMEM((TR_DEV, TILE, 128), f32),
            pltpu.VMEM((2, 9, 128), f32),
            pltpu.VMEM((3, 2, 8, 128), f32),
            pltpu.VMEM((NZ, 9, 128), f32),
            pltpu.VMEM((3, NZ, 8, 128), f32),
            pltpu.VMEM((8, 128), f32),
            pltpu.VMEM((8, 8, 128), f32),
            pltpu.VMEM((NZ, 8, 128), f32),
            pltpu.VMEM((3, 8, 8, 128), f32),
            pltpu.VMEM((3, 8, 8, 128), f32),
            pltpu.VMEM((3, 8, 8, 128), f32),
            pltpu.VMEM((3, 4, 2, 8, 128), f32),
            pltpu.VMEM((2, 8, 128), f32),
            pltpu.VMEM((8, 2, 8, 128), f32),
            pltpu.VMEM((8, 8, 128), f32),
            pltpu.VMEM((8, 8, 8, 128), f32),
            pltpu.VMEM((4, 8, 128), f32),
            pltpu.VMEM((4, 8, 8, 128), f32),
            dma((SLOTS,)),
            dma((4,)),
            dma((4, NZ)),
            dma,
            dma,
            dma((3,)),
            dma((3,)),
            dma((3,)),
            dma((3,)),
            dma,
            dma,
            dma,
            dma,
            dma((4,)),
            dma((4,)),
            pltpu.SemaphoreType.REGULAR,
        ],
        compiler_params=pltpu.CompilerParams(
            collective_id=0, has_side_effects=True, vmem_limit_bytes=52 * 1024 * 1024
        ),
    )(facts, tiles)
    return row_scale.reshape(-1), col_scale.reshape(-1)


def solution(mesh):
    return jax.shard_map(
        on_device,
        mesh=mesh,
        in_specs=(P(("row", "col"), None, None), P(("row", "col"), None), P(("row", "col"))),
        out_specs=(P("row"), P("col")),
        check_vma=False,
    )
```

```python
import functools

import jax
import jax.numpy as jnp
from jax import lax
from jax.experimental import pallas as pl
from jax.experimental.pallas import tpu as pltpu
from jax.sharding import PartitionSpec as P

MESH = pl.DeviceIdType.MESH
TR_DEV = 2
TC_DEV = 32
SLOTS = 4
TILE = 512
EPS = 1e-06
NY, NZ, NX, NC = 4, 16, 4, 2

Z_STEP = [0] + [(q + 1) // 2 if q % 2 else -(q // 2) for q in range(1, NZ)]
Y_STEP = [(dy, p) for dy in (0, 1, 3, 2) for p in (0, 1)]
X_STEP = [(dx, dc) for dx in (0, 1, 3, 2) for dc in (0, 1)]
D_STEP = [0, 1, 3, 2]


def scaled(value, peak):
    return value * lax.rsqrt(value * peak + EPS)


def kernel(
    facts_ref, tiles_ref, row_out, col_out,
    tile, by_row, by_col, fold, z_src0, z_src, z_buf0, z_buf, meta_src, meta_y, meta_z,
    y_src, y_buf, d_src, d_buf, f_src, f_buf, g_src, g_buf, r_src, r_buf,
    load_sem, z_send, z_recv, m_send, m_recv, y_send, y_recv, d_send, d_recv,
    f_send, f_recv, g_send, g_recv, r_send, r_recv,
):
    row, col = lax.axis_index("row"), lax.axis_index("col")
    y, z = row // NZ, lax.rem(row, NZ)
    x, core = col // NC, lax.rem(col, NC)
    half = lax.rem(z, 2)

    def z_peer(q):
        return (y * NZ + lax.rem(z + Z_STEP[q] + NZ, NZ), col)

    def y_peer(j):
        dy, p = Y_STEP[j]
        return (lax.rem(y + dy, NY) * NZ + (z + 1 - 2 * half if p else z), col)

    def x_peer(j):
        dx, dc = X_STEP[j]
        return (row, lax.rem(x + dx, NX) * NC + lax.rem(core + dc, NC))

    def d_peer(j):
        return (lax.rem(y + D_STEP[j], NY) * NZ + z, col)

    def remote(src, dst, send, recv, peer):
        return pltpu.make_async_remote_copy(
            src_ref=src, dst_ref=dst, send_sem=send, recv_sem=recv,
            device_id=peer, device_id_type=MESH,
        )

    barrier = pltpu.get_barrier_semaphore()
    peers = [z_peer(q) for q in range(NZ - 1, 0, -1)]
    peers += [y_peer(j) for j in range(7, 1, -1)]
    peers += [x_peer(j) for j in range(7, 0, -1)]
    for peer in peers:
        pl.semaphore_signal(barrier, inc=1, device_id=peer, device_id_type=MESH)

    loads = [
        pltpu.make_async_copy(tiles_ref.at[s], tile.at[s], load_sem.at[s]) for s in range(SLOTS)
    ]
    for load in loads:
        load.start()

    iota = lax.broadcasted_iota(jnp.int32, (8, 128), 0)
    lane = lax.broadcasted_iota(jnp.int32, (8, 128), 1)

    def wide(value):
        return jnp.broadcast_to(value, (8, 128))

    def tall(value, rows):
        return jnp.broadcast_to(value[None], (rows // 8, 8, 128)).reshape(rows, 128)

    second, in_row = [], []
    meta = jnp.full((8, 128), -1.0, jnp.float32)
    meta_line = jnp.full((1, 128), -1.0, jnp.float32)
    for s in range(SLOTS):
        tile_row = wide(facts_ref[0:1, s : s + 1])
        live = tile_row >= 0
        tile_row = tile_row - row * TR_DEV
        second.append(jnp.where(tile_row > 0, 1.0, 0.0))
        in_row.append(
            [jnp.where(live, jnp.where(tile_row == t, 1.0, 0.0), 0.0) for t in range(TR_DEV)]
        )
        at = jnp.where(live, wide(facts_ref[1:2, s : s + 1]) - col * TC_DEV, -1)
        at = at.astype(jnp.float32)
        meta = jnp.where(iota // 2 == s, at, meta)
        meta_line = jnp.where(lane[0:1] // 2 == s, at[0:1], meta_line)
    meta_src[...] = meta
    for p in range(2):
        z_src0[p, 8:9, :] = meta_line

    def combine(total):
        return (jnp.add, jnp.sum) if total else (jnp.maximum, jnp.max)

    def put_columns(k, s, acc, fold_of):
        for b in range(4):
            line = fold_of(acc[b], axis=0, keepdims=True)
            at = 2 * s + b % 2
            which = half if b // 2 == 0 else 1 - half
            if k == 0:
                z_src0[which, at : at + 1, :] = line
            else:
                z_src[k - 1, which, at : at + 1, :] = line

    def put_rows(k, fold_of):
        res = jnp.zeros((8, 128), jnp.float32)
        for t in range(TR_DEV):
            for blk in range(4):
                line = fold_of(fold[t, blk * 128 : (blk + 1) * 128, :].T, axis=0, keepdims=True)
                res = jnp.where(iota == t * 4 + blk, line, res)
        r_src[k] = res

    zeros = (jnp.zeros((8, 128), jnp.float32),) * 4

    def first_pass():
        for s in range(SLOTS):
            loads[s].wait()

            def body(c, acc):
                start = pl.multiple_of(c * 32, 32)
                acc, part = list(acc), None
                for b in range(4):
                    piece = jnp.abs(tile[s, pl.ds(start, 32), b * 128 : (b + 1) * 128])
                    tile[s, pl.ds(start, 32), b * 128 : (b + 1) * 128] = piece
                    acc[b] = jnp.maximum(acc[b], jnp.max(piece.reshape(4, 8, 128), axis=0))
                    part = piece if part is None else jnp.maximum(part, piece)
                for t in range(TR_DEV):
                    side = jnp.where(tall(in_row[s][t], 32) > 0.5, part, 0.0)
                    if s:
                        side = jnp.maximum(side, fold[t, pl.ds(start, 32), :])
                    fold[t, pl.ds(start, 32), :] = side
                return tuple(acc)

            put_columns(0, s, lax.fori_loop(0, TILE // 32, body, zeros, unroll=2), jnp.max)
        put_rows(0, jnp.max)

    def column_pass(k, total=False):
        join, fold_of = combine(total)
        accs = []
        for s in range(SLOTS):

            def body(c, acc):
                start = pl.multiple_of(c * 64, 64)
                weight = jnp.where(
                    tall(second[s], 64) > 0.5,
                    by_row[1, pl.ds(start, 64), :],
                    by_row[0, pl.ds(start, 64), :],
                )
                acc = list(acc)
                for b in range(4):
                    part = tile[s, pl.ds(start, 64), b * 128 : (b + 1) * 128] * weight
                    acc[b] = join(acc[b], fold_of(part.reshape(8, 8, 128), axis=0))
                return tuple(acc)

            accs.append(lax.fori_loop(0, TILE // 64, body, zeros, unroll=4))
        for s in range(SLOTS):
            put_columns(k, s, accs[s], fold_of)

    def row_pass(k, p, total=False):
        join, fold_of = combine(total)
        left = (half if p == 0 else 1 - half) * 256

        def body(c, carry):
            start = pl.multiple_of(c * 32, 32)
            sides = [None] * TR_DEV
            if p:
                sides = [fold[t, pl.ds(start, 32), :] for t in range(TR_DEV)]
            for s in range(SLOTS):
                part = None
                for b in range(2):
                    at = 2 * s + b
                    lanes = pl.ds(pl.multiple_of(left + b * 128, 128), 128)
                    piece = tile[s, pl.ds(start, 32), lanes] * by_col[p, at : at + 1, :]
                    part = piece if part is None else join(part, piece)
                for t in range(TR_DEV):
                    side = jnp.where(tall(in_row[s][t], 32) > 0.5, part, 0.0)
                    sides[t] = side if sides[t] is None else join(sides[t], side)
            for t in range(TR_DEV):
                fold[t, pl.ds(start, 32), :] = sides[t]
            return carry

        lax.fori_loop(0, TILE // 32, body, 0, unroll=2)
        if p:
            put_rows(k, fold_of)

    def send_rows(k):
        for j in range(7, 0, -1):
            remote(r_src.at[k], r_buf.at[k, j], r_send.at[k], r_recv.at[k], x_peer(j)).start()

    def wait_rows(k, total=False):
        join, _ = combine(total)
        whole = r_buf.at[k, pl.ds(1, 7)]
        remote(whole, whole, r_send.at[k], r_recv.at[k], x_peer(1)).wait_recv()
        out = r_src[k]
        for j in range(1, 8):
            out = join(out, r_buf[k, j])
        return out

    def spread_rows(d):
        for t in range(TR_DEV):
            for blk in range(4):
                at = t * 4 + blk
                wide = jnp.broadcast_to(d[at : at + 1, :], (128, 128))
                by_row[t, blk * 128 : (blk + 1) * 128, :] = wide.T

    def z_refs(k, q):
        if k == 0:
            return z_buf0.at[q]
        return z_buf.at[k - 1, q]

    def z_from(k, p):
        return z_src0.at[p] if k == 0 else z_src.at[k - 1, p]

    def send_z(k):
        for q in range(NZ - 1, 0, -1):
            remote(
                z_from(k, Z_STEP[q] % 2), z_refs(k, q), z_send.at[k], z_recv.at[k, q], z_peer(q)
            ).start()

    def gather_z(k, targets, wait, total=False):
        join, _ = combine(total)

        def add(acc, value, at):
            acc = list(acc)
            for turn in range(4):
                v = pltpu.roll(value, 2 * turn, 0) if turn else value
                m = pltpu.roll(at, 2 * turn, 0) if turn else at
                for j in range(8):
                    acc[j] = join(acc[j], jnp.where(m == targets[j], v, 0.0))
            return tuple(acc)

        def body(q, acc):
            if wait:
                ref = z_refs(k, q)
                remote(ref, ref, z_send.at[k], z_recv.at[k, q], z_peer(1)).wait_recv()
            value = z_buf0[q, 0:8, :] if k == 0 else z_buf[k - 1, q]
            if k == 0 and wait:
                line = jnp.where(lane == iota, z_buf0[q, 8:9, :], -1.0)
                at = jnp.broadcast_to(jnp.max(line, axis=1, keepdims=True), (8, 128))
                meta_z[q] = at
            else:
                at = meta_z[q]
            return add(acc, value, at)

        own = z_src0[0, 0:8, :] if k == 0 else z_src[k - 1, 0]
        acc = add((jnp.zeros((8, 128), jnp.float32),) * 8, own, meta_src[...])
        return lax.fori_loop(1, NZ, body, acc)

    def send_slots(k):
        own = []
        for j in range(1, 8):
            dy, p = Y_STEP[j]
            at = meta_y[Y_STEP.index(((NY - dy) % NY, p))]
            own.append(jnp.where(at < 0, -2.0, at))
        first = jnp.where(meta_src[...] < 0, -2.0, meta_src[...])
        acc = gather_z(k, [first] + own, True)
        for j in range(8):
            y_src[k, j] = acc[j]
        for j in range(7, 0, -1):
            remote(
                y_src.at[k, j], y_buf.at[k, j % 2, j // 2], y_send.at[k], y_recv.at[k, j % 2],
                y_peer(j),
            ).start()

    def wait_slots(k, p):
        whole = y_buf.at[k, 1] if p else y_buf.at[k, 0, pl.ds(1, 3)]
        remote(whole, whole, y_send.at[k], y_recv.at[k, p], y_peer(1)).wait_recv()
        out = y_buf[k, 1, 0] if p else y_src[k, 0]
        for n in range(1, 4):
            out = jnp.maximum(out, y_buf[k, p, n])
        return out

    def next_rows(k, before, k_row, total=False):
        after = []
        for p in range(2):
            e = scaled(before[p], wait_slots(k, p))
            by_col[p] = e
            row_pass(k_row, p, total)
            after.append(e)
        send_rows(k_row)
        return after

    def dense(k, wait=False, total=False):
        every = [(4 * j + iota // 2).astype(jnp.float32) for j in range(8)]
        return gather_z(k, every, wait, total)

    def send_dense(k):
        for j, acc in enumerate(dense(k)):
            d_src[k, j] = acc
        for j in range(3, 0, -1):
            there = lax.rem(y + D_STEP[j], NY)
            remote(
                d_src.at[k, pl.ds(2 * there, 2)], d_buf.at[k, j], d_send.at[k], d_recv.at[k],
                d_peer(j),
            ).start()

    def send_totals():
        for j, acc in enumerate(dense(3, wait=True, total=True)):
            g_src[j] = acc
        for j in range(7, 0, -1):
            remote(g_src, g_buf.at[j], g_send, g_recv, y_peer(j)).start()

    def wait_dense(k):
        whole = d_buf.at[k, pl.ds(1, 3)]
        remote(whole, whole, d_send.at[k], d_recv.at[k], d_peer(1)).wait_recv()
        out = d_src[k, pl.ds(2 * y, 2)]
        for j in range(1, 4):
            out = jnp.maximum(out, d_buf[k, j])
        return out

    def columns_out():
        whole = f_buf.at[pl.ds(1, 7)]
        remote(whole, whole, f_send, f_recv, y_peer(1)).wait_recv()
        whole = g_buf.at[pl.ds(1, 7)]
        remote(whole, whole, g_send, g_recv, y_peer(1)).wait_recv()
        for g in range(4):
            dy = Y_STEP[2 * g][0]
            there = lax.rem(y - dy + NY, NY)
            for n in range(2):
                at = 2 * there + n
                sums = [g_src[at], g_buf[1, at]]
                for j in range(2, 8):
                    sums[j % 2] = sums[j % 2] + g_buf[j, at]
                near = scaled(f_src[n] if g == 0 else f_buf[2 * g, n], sums[0])
                far = scaled(f_buf[2 * g + 1, n], sums[1])
                low = jnp.where(half == 0, near, far)
                high = jnp.where(half == 0, far, near)
                for s in range(4):
                    at = (s % 2) * 4
                    col_out[there * 4 + n * 2 + s // 2, at : at + 2, :] = low[2 * s : 2 * s + 2, :]
                    col_out[there * 4 + n * 2 + s // 2, at + 2 : at + 4, :] = high[2 * s : 2 * s + 2, :]

    def wait_sends():
        for k in range(4):
            ref = z_buf0.at[pl.ds(1, 15)] if k == 0 else z_buf.at[k - 1, pl.ds(1, 15)]
            remote(ref, ref, z_send.at[k], z_recv.at[k, 1], z_peer(1)).wait_send()
            ref = r_buf.at[k, pl.ds(1, 7)]
            remote(ref, ref, r_send.at[k], r_recv.at[k], x_peer(1)).wait_send()
        for k in range(3):
            ref = d_buf.at[k, pl.ds(1, 3)]
            remote(ref, ref, d_send.at[k], d_recv.at[k], d_peer(1)).wait_send()
            ref = meta_y.at[pl.ds(1, 7)]
            remote(ref, ref, y_send.at[k], y_recv.at[k, 0], y_peer(1)).wait_send()
        ref = meta_y.at[pl.ds(1, 7)]
        remote(ref, ref, m_send, m_recv, y_peer(1)).wait_send()
        ref = f_buf.at[pl.ds(1, 7)]
        remote(ref, ref, f_send, f_recv, y_peer(1)).wait_send()
        ref = g_buf.at[pl.ds(1, 7)]
        remote(ref, ref, g_send, g_recv, y_peer(1)).wait_send()

    one = jnp.ones((8, 128), jnp.float32)
    first_pass()
    pl.semaphore_wait(barrier, len(peers))
    send_rows(0)
    send_z(0)
    for j in range(7, 0, -1):
        remote(meta_src, meta_y.at[j], m_send, m_recv, y_peer(j)).start()
    peak = wait_rows(0)
    d1 = scaled(one, peak)
    spread_rows(d1)
    column_pass(1)
    send_z(1)
    whole = meta_y.at[pl.ds(1, 7)]
    remote(whole, whole, m_send, m_recv, y_peer(1)).wait_recv()
    send_slots(0)
    send_dense(0)
    send_slots(1)
    e1 = next_rows(0, [one, one], 1)
    send_dense(1)
    e2 = next_rows(1, e1, 2)
    peak = wait_rows(1)
    d2 = scaled(d1, peak)
    spread_rows(d2)
    column_pass(2)
    send_z(2)
    peak = wait_rows(2)
    d3 = scaled(d2, peak)
    spread_rows(d3)
    column_pass(3, total=True)
    send_z(3)
    send_slots(2)
    send_dense(2)
    send_totals()
    mine = jnp.ones((2, 8, 128), jnp.float32)
    for k in range(3):
        mine = scaled(mine, wait_dense(k))
    f_src[...] = mine
    for j in range(7, 0, -1):
        remote(f_src, f_buf.at[j], f_send, f_recv, y_peer(j)).start()
    next_rows(2, e2, 3, total=True)
    columns_out()
    row_out[...] = scaled(d3, wait_rows(3, total=True))
    wait_sends()

def on_device(tiles, tile_list, tile_count):
    f32 = jnp.float32
    live = jnp.arange(SLOTS, dtype=jnp.int32)[None, :] < tile_count[:, None]
    facts = jnp.where(live, tile_list.T, -1)
    dma = pltpu.SemaphoreType.DMA
    row_scale, col_scale = pl.pallas_call(
        kernel,
        out_shape=(
            jax.ShapeDtypeStruct((8, 128), f32),
            jax.ShapeDtypeStruct((16, 8, 128), f32),
        ),
        in_specs=[
            pl.BlockSpec(memory_space=pltpu.VMEM),
            pl.BlockSpec(memory_space=pl.ANY),
        ],
        out_specs=(
            pl.BlockSpec(memory_space=pltpu.VMEM),
            pl.BlockSpec(memory_space=pltpu.VMEM),
        ),
        scratch_shapes=[
            pltpu.VMEM((SLOTS, TILE, TILE), f32),
            pltpu.VMEM((TR_DEV, TILE, 128), f32),
            pltpu.VMEM((2, 8, 128), f32),
            pltpu.VMEM((TR_DEV, TILE, 128), f32),
            pltpu.VMEM((2, 9, 128), f32),
            pltpu.VMEM((3, 2, 8, 128), f32),
            pltpu.VMEM((NZ, 9, 128), f32),
            pltpu.VMEM((3, NZ, 8, 128), f32),
            pltpu.VMEM((8, 128), f32),
            pltpu.VMEM((8, 8, 128), f32),
            pltpu.VMEM((NZ, 8, 128), f32),
            pltpu.VMEM((3, 8, 8, 128), f32),
            pltpu.VMEM((3, 2, 4, 8, 128), f32),
            pltpu.VMEM((3, 8, 8, 128), f32),
            pltpu.VMEM((3, 4, 2, 8, 128), f32),
            pltpu.VMEM((2, 8, 128), f32),
            pltpu.VMEM((8, 2, 8, 128), f32),
            pltpu.VMEM((8, 8, 128), f32),
            pltpu.VMEM((8, 8, 8, 128), f32),
            pltpu.VMEM((4, 8, 128), f32),
            pltpu.VMEM((4, 8, 8, 128), f32),
            dma((SLOTS,)),
            dma((4,)),
            dma((4, NZ)),
            dma,
            dma,
            dma((3,)),
            dma((3, 2)),
            dma((3,)),
            dma((3,)),
            dma,
            dma,
            dma,
            dma,
            dma((4,)),
            dma((4,)),
        ],
        compiler_params=pltpu.CompilerParams(
            collective_id=0, has_side_effects=True, vmem_limit_bytes=52 * 1024 * 1024
        ),
    )(facts, tiles)
    return row_scale.reshape(-1), col_scale.reshape(-1)


def solution(mesh):
    return jax.shard_map(
        on_device,
        mesh=mesh,
        in_specs=(P(("row", "col"), None, None), P(("row", "col"), None), P(("row", "col"))),
        out_specs=(P("row"), P("col")),
        check_vma=False,
    )
```

```python
import functools

import jax
import jax.numpy as jnp
from jax import lax
from jax.experimental import pallas as pl
from jax.experimental.pallas import tpu as pltpu
from jax.sharding import PartitionSpec as P

MESH = pl.DeviceIdType.MESH
TR_DEV = 2
TC_DEV = 32
SLOTS = 4
TILE = 512
EPS = 1e-06
NY, NZ, NX, NC = 4, 16, 4, 2

Z_STEP = [0] + [(q + 1) // 2 if q % 2 else -(q // 2) for q in range(1, NZ)]
Y_STEP = [(dy, p) for dy in (0, 1, 3, 2) for p in (0, 1)]
X_STEP = [(dx, dc) for dx in (0, 1, 3, 2) for dc in (0, 1)]
D_STEP = [0, 1, 3, 2]


def scaled(value, peak):
    return value * lax.rsqrt(value * peak + EPS)


def kernel(
    facts_ref, tiles_ref, row_out, col_out,
    tile, by_row, by_col, fold, z_src0, z_src, z_buf0, z_buf, meta_src, meta_y, meta_z,
    y_src, y_buf, d_src, d_buf, f_src, f_buf, g_src, g_buf, r_src, r_buf,
    load_sem, z_send, z_recv, m_send, m_recv, y_send, y_recv, d_send, d_recv,
    f_send, f_recv, g_send, g_recv, r_send, r_recv,
):
    row, col = lax.axis_index("row"), lax.axis_index("col")
    y, z = row // NZ, lax.rem(row, NZ)
    x, core = col // NC, lax.rem(col, NC)
    half = lax.rem(z, 2)

    def z_peer(q):
        return (y * NZ + lax.rem(z + Z_STEP[q] + NZ, NZ), col)

    def y_peer(j):
        dy, p = Y_STEP[j]
        return (lax.rem(y + dy, NY) * NZ + (z + 1 - 2 * half if p else z), col)

    def x_peer(j):
        dx, dc = X_STEP[j]
        return (row, lax.rem(x + dx, NX) * NC + lax.rem(core + dc, NC))

    def d_peer(j):
        return (lax.rem(y + D_STEP[j], NY) * NZ + z, col)

    def remote(src, dst, send, recv, peer):
        return pltpu.make_async_remote_copy(
            src_ref=src, dst_ref=dst, send_sem=send, recv_sem=recv,
            device_id=peer, device_id_type=MESH,
        )

    barrier = pltpu.get_barrier_semaphore()
    peers = [z_peer(q) for q in range(NZ - 1, 0, -1)]
    peers += [y_peer(j) for j in range(7, 1, -1)]
    peers += [x_peer(j) for j in range(7, 0, -1)]
    for peer in peers:
        pl.semaphore_signal(barrier, inc=1, device_id=peer, device_id_type=MESH)

    loads = [
        pltpu.make_async_copy(tiles_ref.at[s], tile.at[s], load_sem.at[s]) for s in range(SLOTS)
    ]
    for load in loads:
        load.start()

    iota = lax.broadcasted_iota(jnp.int32, (8, 128), 0)
    lane = lax.broadcasted_iota(jnp.int32, (8, 128), 1)

    def wide(value):
        return jnp.broadcast_to(value, (8, 128))

    def tall(value, rows):
        return jnp.broadcast_to(value[None], (rows // 8, 8, 128)).reshape(rows, 128)

    second, in_row = [], []
    meta = jnp.full((8, 128), -1.0, jnp.float32)
    meta_line = jnp.full((1, 128), -1.0, jnp.float32)
    for s in range(SLOTS):
        tile_row = wide(facts_ref[0:1, s : s + 1])
        live = tile_row >= 0
        tile_row = tile_row - row * TR_DEV
        second.append(jnp.where(tile_row > 0, 1.0, 0.0))
        in_row.append(
            [jnp.where(live, jnp.where(tile_row == t, 1.0, 0.0), 0.0) for t in range(TR_DEV)]
        )
        at = jnp.where(live, wide(facts_ref[1:2, s : s + 1]) - col * TC_DEV, -1)
        at = at.astype(jnp.float32)
        meta = jnp.where(iota // 2 == s, at, meta)
        meta_line = jnp.where(lane[0:1] // 2 == s, at[0:1], meta_line)
    meta_src[...] = meta
    for p in range(2):
        z_src0[p, 8:9, :] = meta_line

    def combine(total):
        return (jnp.add, jnp.sum) if total else (jnp.maximum, jnp.max)

    def put_columns(k, s, acc, fold_of):
        for b in range(4):
            line = fold_of(acc[b], axis=0, keepdims=True)
            at = 2 * s + b % 2
            which = half if b // 2 == 0 else 1 - half
            if k == 0:
                z_src0[which, at : at + 1, :] = line
            else:
                z_src[k - 1, which, at : at + 1, :] = line

    def put_rows(k, fold_of):
        res = jnp.zeros((8, 128), jnp.float32)
        for t in range(TR_DEV):
            for blk in range(4):
                line = fold_of(fold[t, blk * 128 : (blk + 1) * 128, :].T, axis=0, keepdims=True)
                res = jnp.where(iota == t * 4 + blk, line, res)
        r_src[k] = res

    zeros = (jnp.zeros((8, 128), jnp.float32),) * 4

    def first_pass():
        for s in range(SLOTS):
            loads[s].wait()

            def body(c, acc):
                start = pl.multiple_of(c * 32, 32)
                acc, part = list(acc), None
                for b in range(4):
                    piece = jnp.abs(tile[s, pl.ds(start, 32), b * 128 : (b + 1) * 128])
                    tile[s, pl.ds(start, 32), b * 128 : (b + 1) * 128] = piece
                    acc[b] = jnp.maximum(acc[b], jnp.max(piece.reshape(4, 8, 128), axis=0))
                    part = piece if part is None else jnp.maximum(part, piece)
                for t in range(TR_DEV):
                    side = jnp.where(tall(in_row[s][t], 32) > 0.5, part, 0.0)
                    if s:
                        side = jnp.maximum(side, fold[t, pl.ds(start, 32), :])
                    fold[t, pl.ds(start, 32), :] = side
                return tuple(acc)

            put_columns(0, s, lax.fori_loop(0, TILE // 32, body, zeros, unroll=2), jnp.max)
        put_rows(0, jnp.max)

    def column_pass(k, total=False):
        join, fold_of = combine(total)
        accs = []
        for s in range(SLOTS):

            def body(c, acc):
                start = pl.multiple_of(c * 64, 64)
                weight = jnp.where(
                    tall(second[s], 64) > 0.5,
                    by_row[1, pl.ds(start, 64), :],
                    by_row[0, pl.ds(start, 64), :],
                )
                acc = list(acc)
                for b in range(4):
                    part = tile[s, pl.ds(start, 64), b * 128 : (b + 1) * 128] * weight
                    acc[b] = join(acc[b], fold_of(part.reshape(8, 8, 128), axis=0))
                return tuple(acc)

            accs.append(lax.fori_loop(0, TILE // 64, body, zeros, unroll=4))
        for s in range(SLOTS):
            put_columns(k, s, accs[s], fold_of)

    def row_pass(k, p, total=False):
        join, fold_of = combine(total)
        left = (half if p == 0 else 1 - half) * 256

        def body(c, carry):
            start = pl.multiple_of(c * 32, 32)
            sides = [None] * TR_DEV
            if p:
                sides = [fold[t, pl.ds(start, 32), :] for t in range(TR_DEV)]
            for s in range(SLOTS):
                part = None
                for b in range(2):
                    at = 2 * s + b
                    lanes = pl.ds(pl.multiple_of(left + b * 128, 128), 128)
                    piece = tile[s, pl.ds(start, 32), lanes] * by_col[p, at : at + 1, :]
                    part = piece if part is None else join(part, piece)
                for t in range(TR_DEV):
                    side = jnp.where(tall(in_row[s][t], 32) > 0.5, part, 0.0)
                    sides[t] = side if sides[t] is None else join(sides[t], side)
            for t in range(TR_DEV):
                fold[t, pl.ds(start, 32), :] = sides[t]
            return carry

        lax.fori_loop(0, TILE // 32, body, 0, unroll=2)
        if p:
            put_rows(k, fold_of)

    def send_rows(k):
        for j in range(7, 0, -1):
            remote(r_src.at[k], r_buf.at[k, j], r_send.at[k], r_recv.at[k], x_peer(j)).start()

    def wait_rows(k, total=False):
        join, _ = combine(total)
        whole = r_buf.at[k, pl.ds(1, 7)]
        remote(whole, whole, r_send.at[k], r_recv.at[k], x_peer(1)).wait_recv()
        out = r_src[k]
        for j in range(1, 8):
            out = join(out, r_buf[k, j])
        return out

    def spread_rows(d):
        for t in range(TR_DEV):
            for blk in range(4):
                at = t * 4 + blk
                wide = jnp.broadcast_to(d[at : at + 1, :], (128, 128))
                by_row[t, blk * 128 : (blk + 1) * 128, :] = wide.T

    def z_refs(k, q):
        if k == 0:
            return z_buf0.at[q]
        return z_buf.at[k - 1, q]

    def z_from(k, p):
        return z_src0.at[p] if k == 0 else z_src.at[k - 1, p]

    def send_z(k):
        for q in range(NZ - 1, 0, -1):
            remote(
                z_from(k, Z_STEP[q] % 2), z_refs(k, q), z_send.at[k], z_recv.at[k, q], z_peer(q)
            ).start()

    def gather_z(k, targets, wait, total=False):
        join, _ = combine(total)

        def add(acc, value, at):
            acc = list(acc)
            for turn in range(4):
                v = pltpu.roll(value, 2 * turn, 0) if turn else value
                m = pltpu.roll(at, 2 * turn, 0) if turn else at
                for j in range(8):
                    acc[j] = join(acc[j], jnp.where(m == targets[j], v, 0.0))
            return tuple(acc)

        def body(q, acc):
            if wait:
                ref = z_refs(k, q)
                remote(ref, ref, z_send.at[k], z_recv.at[k, q], z_peer(1)).wait_recv()
            value = z_buf0[q, 0:8, :] if k == 0 else z_buf[k - 1, q]
            if k == 0 and wait:
                line = jnp.where(lane == iota, z_buf0[q, 8:9, :], -1.0)
                at = jnp.broadcast_to(jnp.max(line, axis=1, keepdims=True), (8, 128))
                meta_z[q] = at
            else:
                at = meta_z[q]
            return add(acc, value, at)

        own = z_src0[0, 0:8, :] if k == 0 else z_src[k - 1, 0]
        acc = add((jnp.zeros((8, 128), jnp.float32),) * 8, own, meta_src[...])
        return lax.fori_loop(1, NZ, body, acc)

    def send_slots(k):
        own = []
        for j in range(1, 8):
            dy, p = Y_STEP[j]
            at = meta_y[Y_STEP.index(((NY - dy) % NY, p))]
            own.append(jnp.where(at < 0, -2.0, at))
        first = jnp.where(meta_src[...] < 0, -2.0, meta_src[...])
        acc = gather_z(k, [first] + own, True)
        for j in range(8):
            y_src[k, j] = acc[j]
        for j in range(7, 0, -1):
            remote(
                y_src.at[k, j], y_buf.at[k, j % 2, j // 2], y_send.at[k], y_recv.at[k, j % 2],
                y_peer(j),
            ).start()

    def wait_slots(k, p):
        whole = y_buf.at[k, 1] if p else y_buf.at[k, 0, pl.ds(1, 3)]
        remote(whole, whole, y_send.at[k], y_recv.at[k, p], y_peer(1)).wait_recv()
        out = y_buf[k, 1, 0] if p else y_src[k, 0]
        for n in range(1, 4):
            out = jnp.maximum(out, y_buf[k, p, n])
        return out

    def next_rows(k, before, k_row, total=False):
        after = []
        for p in range(2):
            e = scaled(before[p], wait_slots(k, p))
            by_col[p] = e
            row_pass(k_row, p, total)
            after.append(e)
        send_rows(k_row)
        return after

    def dense(k, wait=False, total=False):
        every = [(4 * j + iota // 2).astype(jnp.float32) for j in range(8)]
        return gather_z(k, every, wait, total)

    def send_dense(k):
        for j, acc in enumerate(dense(k)):
            d_src[k, j] = acc
        for j in range(3, 0, -1):
            there = lax.rem(y + D_STEP[j], NY)
            remote(
                d_src.at[k, pl.ds(2 * there, 2)], d_buf.at[k, j], d_send.at[k], d_recv.at[k],
                d_peer(j),
            ).start()

    def send_totals():
        for j, acc in enumerate(dense(3, wait=True, total=True)):
            g_src[j] = acc
        for j in range(7, 0, -1):
            remote(g_src, g_buf.at[j], g_send, g_recv, y_peer(j)).start()

    def wait_dense(k):
        whole = d_buf.at[k, pl.ds(1, 3)]
        remote(whole, whole, d_send.at[k], d_recv.at[k], d_peer(1)).wait_recv()
        out = d_src[k, pl.ds(2 * y, 2)]
        for j in range(1, 4):
            out = jnp.maximum(out, d_buf[k, j])
        return out

    def columns_out():
        whole = f_buf.at[pl.ds(1, 7)]
        remote(whole, whole, f_send, f_recv, y_peer(1)).wait_recv()
        whole = g_buf.at[pl.ds(1, 7)]
        remote(whole, whole, g_send, g_recv, y_peer(1)).wait_recv()
        for g in range(4):
            dy = Y_STEP[2 * g][0]
            there = lax.rem(y - dy + NY, NY)
            for n in range(2):
                at = 2 * there + n
                sums = [g_src[at], g_buf[1, at]]
                for j in range(2, 8):
                    sums[j % 2] = sums[j % 2] + g_buf[j, at]
                near = scaled(f_src[n] if g == 0 else f_buf[2 * g, n], sums[0])
                far = scaled(f_buf[2 * g + 1, n], sums[1])
                low = jnp.where(half == 0, near, far)
                high = jnp.where(half == 0, far, near)
                for s in range(4):
                    at = (s % 2) * 4
                    col_out[there * 4 + n * 2 + s // 2, at : at + 2, :] = low[2 * s : 2 * s + 2, :]
                    col_out[there * 4 + n * 2 + s // 2, at + 2 : at + 4, :] = high[2 * s : 2 * s + 2, :]

    def wait_sends():
        for k in range(4):
            ref = z_buf0.at[pl.ds(1, 15)] if k == 0 else z_buf.at[k - 1, pl.ds(1, 15)]
            remote(ref, ref, z_send.at[k], z_recv.at[k, 1], z_peer(1)).wait_send()
            ref = r_buf.at[k, pl.ds(1, 7)]
            remote(ref, ref, r_send.at[k], r_recv.at[k], x_peer(1)).wait_send()
        for k in range(3):
            ref = d_buf.at[k, pl.ds(1, 3)]
            remote(ref, ref, d_send.at[k], d_recv.at[k], d_peer(1)).wait_send()
            ref = meta_y.at[pl.ds(1, 7)]
            remote(ref, ref, y_send.at[k], y_recv.at[k, 0], y_peer(1)).wait_send()
        ref = meta_y.at[pl.ds(1, 7)]
        remote(ref, ref, m_send, m_recv, y_peer(1)).wait_send()
        ref = f_buf.at[pl.ds(1, 7)]
        remote(ref, ref, f_send, f_recv, y_peer(1)).wait_send()
        ref = g_buf.at[pl.ds(1, 7)]
        remote(ref, ref, g_send, g_recv, y_peer(1)).wait_send()

    one = jnp.ones((8, 128), jnp.float32)
    first_pass()
    pl.semaphore_wait(barrier, len(peers))
    send_rows(0)
    send_z(0)
    for j in range(7, 0, -1):
        remote(meta_src, meta_y.at[j], m_send, m_recv, y_peer(j)).start()
    peak = wait_rows(0)
    d1 = scaled(one, peak)
    spread_rows(d1)
    column_pass(1)
    send_z(1)
    whole = meta_y.at[pl.ds(1, 7)]
    remote(whole, whole, m_send, m_recv, y_peer(1)).wait_recv()
    send_slots(0)
    send_dense(0)
    send_slots(1)
    e1 = next_rows(0, [one, one], 1)
    send_dense(1)
    e2 = next_rows(1, e1, 2)
    peak = wait_rows(1)
    d2 = scaled(d1, peak)
    spread_rows(d2)
    column_pass(2)
    send_z(2)
    peak = wait_rows(2)
    d3 = scaled(d2, peak)
    spread_rows(d3)
    column_pass(3, total=True)
    send_z(3)
    send_slots(2)
    send_dense(2)
    mine = jnp.ones((2, 8, 128), jnp.float32)
    for k in range(3):
        mine = scaled(mine, wait_dense(k))
    f_src[...] = mine
    for j in range(7, 0, -1):
        remote(f_src, f_buf.at[j], f_send, f_recv, y_peer(j)).start()
    send_totals()
    next_rows(2, e2, 3, total=True)
    columns_out()
    row_out[...] = scaled(d3, wait_rows(3, total=True))
    wait_sends()

def on_device(tiles, tile_list, tile_count):
    f32 = jnp.float32
    live = jnp.arange(SLOTS, dtype=jnp.int32)[None, :] < tile_count[:, None]
    facts = jnp.where(live, tile_list.T, -1)
    dma = pltpu.SemaphoreType.DMA
    row_scale, col_scale = pl.pallas_call(
        kernel,
        out_shape=(
            jax.ShapeDtypeStruct((8, 128), f32),
            jax.ShapeDtypeStruct((16, 8, 128), f32),
        ),
        in_specs=[
            pl.BlockSpec(memory_space=pltpu.VMEM),
            pl.BlockSpec(memory_space=pl.ANY),
        ],
        out_specs=(
            pl.BlockSpec(memory_space=pltpu.VMEM),
            pl.BlockSpec(memory_space=pltpu.VMEM),
        ),
        scratch_shapes=[
            pltpu.VMEM((SLOTS, TILE, TILE), f32),
            pltpu.VMEM((TR_DEV, TILE, 128), f32),
            pltpu.VMEM((2, 8, 128), f32),
            pltpu.VMEM((TR_DEV, TILE, 128), f32),
            pltpu.VMEM((2, 9, 128), f32),
            pltpu.VMEM((3, 2, 8, 128), f32),
            pltpu.VMEM((NZ, 9, 128), f32),
            pltpu.VMEM((3, NZ, 8, 128), f32),
            pltpu.VMEM((8, 128), f32),
            pltpu.VMEM((8, 8, 128), f32),
            pltpu.VMEM((NZ, 8, 128), f32),
            pltpu.VMEM((3, 8, 8, 128), f32),
            pltpu.VMEM((3, 2, 4, 8, 128), f32),
            pltpu.VMEM((3, 8, 8, 128), f32),
            pltpu.VMEM((3, 4, 2, 8, 128), f32),
            pltpu.VMEM((2, 8, 128), f32),
            pltpu.VMEM((8, 2, 8, 128), f32),
            pltpu.VMEM((8, 8, 128), f32),
            pltpu.VMEM((8, 8, 8, 128), f32),
            pltpu.VMEM((4, 8, 128), f32),
            pltpu.VMEM((4, 8, 8, 128), f32),
            dma((SLOTS,)),
            dma((4,)),
            dma((4, NZ)),
            dma,
            dma,
            dma((3,)),
            dma((3, 2)),
            dma((3,)),
            dma((3,)),
            dma,
            dma,
            dma,
            dma,
            dma((4,)),
            dma((4,)),
        ],
        compiler_params=pltpu.CompilerParams(
            collective_id=0, has_side_effects=True, vmem_limit_bytes=52 * 1024 * 1024
        ),
    )(facts, tiles)
    return row_scale.reshape(-1), col_scale.reshape(-1)


def solution(mesh):
    return jax.shard_map(
        on_device,
        mesh=mesh,
        in_specs=(P(("row", "col"), None, None), P(("row", "col"), None), P(("row", "col"))),
        out_specs=(P("row"), P("col")),
        check_vma=False,
    )
```

```python
import functools

import jax
import jax.numpy as jnp
from jax import lax
from jax.experimental import pallas as pl
from jax.experimental.pallas import tpu as pltpu
from jax.sharding import PartitionSpec as P

MESH = pl.DeviceIdType.MESH
TR_DEV = 2
TC_DEV = 32
SLOTS = 4
TILE = 512
EPS = 1e-06
NY, NZ, NX, NC = 4, 16, 4, 2

Z_STEP = [0] + [(q + 1) // 2 if q % 2 else -(q // 2) for q in range(1, NZ)]
Y_STEP = [(dy, p) for dy in (0, 1, 3, 2) for p in (0, 1)]
X_STEP = [(dx, dc) for dx in (0, 1, 3, 2) for dc in (0, 1)]
D_STEP = [0, 1, 3, 2]


def scaled(value, peak):
    return value * lax.rsqrt(value * peak + EPS)


def kernel(
    facts_ref, tiles_ref, row_out, col_out,
    tile, by_row, by_col, fold, z_src0, z_src, z_buf0, z_buf, meta_src, meta_y, meta_z,
    y_src, y_buf, d_src, d_buf, f_src, f_buf, g_src, g_buf, r_src, r_buf,
    load_sem, z_send, z_recv, m_send, m_recv, y_send, y_recv, d_send, d_recv,
    f_send, f_recv, g_send, g_recv, r_send, r_recv, far_sem,
):
    row, col = lax.axis_index("row"), lax.axis_index("col")
    y, z = row // NZ, lax.rem(row, NZ)
    x, core = col // NC, lax.rem(col, NC)
    half = lax.rem(z, 2)

    def z_peer(q):
        return (y * NZ + lax.rem(z + Z_STEP[q] + NZ, NZ), col)

    def y_peer(j):
        dy, p = Y_STEP[j]
        return (lax.rem(y + dy, NY) * NZ + (z + 1 - 2 * half if p else z), col)

    def x_peer(j):
        dx, dc = X_STEP[j]
        return (row, lax.rem(x + dx, NX) * NC + lax.rem(core + dc, NC))

    def d_peer(j):
        return (lax.rem(y + D_STEP[j], NY) * NZ + z, col)

    def remote(src, dst, send, recv, peer):
        return pltpu.make_async_remote_copy(
            src_ref=src, dst_ref=dst, send_sem=send, recv_sem=recv,
            device_id=peer, device_id_type=MESH,
        )

    barrier = pltpu.get_barrier_semaphore()
    peers = [z_peer(q) for q in range(8, 0, -1)]
    peers += [y_peer(j) for j in range(7, 1, -1)]
    peers += [x_peer(j) for j in range(7, 0, -1)]
    for peer in peers:
        pl.semaphore_signal(barrier, inc=1, device_id=peer, device_id_type=MESH)

    loads = [
        pltpu.make_async_copy(tiles_ref.at[s], tile.at[s], load_sem.at[s]) for s in range(SLOTS)
    ]
    for load in loads:
        load.start()

    iota = lax.broadcasted_iota(jnp.int32, (8, 128), 0)
    lane = lax.broadcasted_iota(jnp.int32, (8, 128), 1)

    def wide(value):
        return jnp.broadcast_to(value, (8, 128))

    def tall(value, rows):
        return jnp.broadcast_to(value[None], (rows // 8, 8, 128)).reshape(rows, 128)

    second, in_row = [], []
    meta = jnp.full((8, 128), -1.0, jnp.float32)
    meta_line = jnp.full((1, 128), -1.0, jnp.float32)
    for s in range(SLOTS):
        tile_row = wide(facts_ref[0:1, s : s + 1])
        live = tile_row >= 0
        tile_row = tile_row - row * TR_DEV
        second.append(jnp.where(tile_row > 0, 1.0, 0.0))
        in_row.append(
            [jnp.where(live, jnp.where(tile_row == t, 1.0, 0.0), 0.0) for t in range(TR_DEV)]
        )
        at = jnp.where(live, wide(facts_ref[1:2, s : s + 1]) - col * TC_DEV, -1)
        at = at.astype(jnp.float32)
        meta = jnp.where(iota // 2 == s, at, meta)
        meta_line = jnp.where(lane[0:1] // 2 == s, at[0:1], meta_line)
    meta_src[...] = meta
    for p in range(2):
        z_src0[p, 8:9, :] = meta_line

    def combine(total):
        return (jnp.add, jnp.sum) if total else (jnp.maximum, jnp.max)

    def put_columns(k, s, acc, fold_of):
        for b in range(4):
            line = fold_of(acc[b], axis=0, keepdims=True)
            at = 2 * s + b % 2
            which = half if b // 2 == 0 else 1 - half
            if k == 0:
                z_src0[which, at : at + 1, :] = line
            else:
                z_src[k - 1, which, at : at + 1, :] = line

    def put_rows(k, fold_of):
        res = jnp.zeros((8, 128), jnp.float32)
        for t in range(TR_DEV):
            for blk in range(4):
                line = fold_of(fold[t, blk * 128 : (blk + 1) * 128, :].T, axis=0, keepdims=True)
                res = jnp.where(iota == t * 4 + blk, line, res)
        r_src[k] = res

    zeros = (jnp.zeros((8, 128), jnp.float32),) * 4

    def first_pass():
        for s in range(SLOTS):
            loads[s].wait()

            def body(c, acc):
                start = pl.multiple_of(c * 32, 32)
                acc, part = list(acc), None
                for b in range(4):
                    piece = jnp.abs(tile[s, pl.ds(start, 32), b * 128 : (b + 1) * 128])
                    tile[s, pl.ds(start, 32), b * 128 : (b + 1) * 128] = piece
                    acc[b] = jnp.maximum(acc[b], jnp.max(piece.reshape(4, 8, 128), axis=0))
                    part = piece if part is None else jnp.maximum(part, piece)
                for t in range(TR_DEV):
                    side = jnp.where(tall(in_row[s][t], 32) > 0.5, part, 0.0)
                    if s:
                        side = jnp.maximum(side, fold[t, pl.ds(start, 32), :])
                    fold[t, pl.ds(start, 32), :] = side
                return tuple(acc)

            put_columns(0, s, lax.fori_loop(0, TILE // 32, body, zeros, unroll=2), jnp.max)
        put_rows(0, jnp.max)

    def column_pass(k, total=False):
        join, fold_of = combine(total)
        accs = []
        for s in range(SLOTS):

            def body(c, acc):
                start = pl.multiple_of(c * 64, 64)
                weight = jnp.where(
                    tall(second[s], 64) > 0.5,
                    by_row[1, pl.ds(start, 64), :],
                    by_row[0, pl.ds(start, 64), :],
                )
                acc = list(acc)
                for b in range(4):
                    part = tile[s, pl.ds(start, 64), b * 128 : (b + 1) * 128] * weight
                    acc[b] = join(acc[b], fold_of(part.reshape(8, 8, 128), axis=0))
                return tuple(acc)

            accs.append(lax.fori_loop(0, TILE // 64, body, zeros, unroll=4))
        for s in range(SLOTS):
            put_columns(k, s, accs[s], fold_of)

    def row_pass(k, p, total=False):
        join, fold_of = combine(total)
        left = (half if p == 0 else 1 - half) * 256

        def body(c, carry):
            start = pl.multiple_of(c * 32, 32)
            sides = [None] * TR_DEV
            if p:
                sides = [fold[t, pl.ds(start, 32), :] for t in range(TR_DEV)]
            for s in range(SLOTS):
                part = None
                for b in range(2):
                    at = 2 * s + b
                    lanes = pl.ds(pl.multiple_of(left + b * 128, 128), 128)
                    piece = tile[s, pl.ds(start, 32), lanes] * by_col[p, at : at + 1, :]
                    part = piece if part is None else join(part, piece)
                for t in range(TR_DEV):
                    side = jnp.where(tall(in_row[s][t], 32) > 0.5, part, 0.0)
                    sides[t] = side if sides[t] is None else join(sides[t], side)
            for t in range(TR_DEV):
                fold[t, pl.ds(start, 32), :] = sides[t]
            return carry

        lax.fori_loop(0, TILE // 32, body, 0, unroll=2)
        if p:
            put_rows(k, fold_of)

    def send_rows(k):
        for j in range(7, 0, -1):
            remote(r_src.at[k], r_buf.at[k, j], r_send.at[k], r_recv.at[k], x_peer(j)).start()

    def wait_rows(k, total=False):
        join, _ = combine(total)
        whole = r_buf.at[k, pl.ds(1, 7)]
        remote(whole, whole, r_send.at[k], r_recv.at[k], x_peer(1)).wait_recv()
        out = r_src[k]
        for j in range(1, 8):
            out = join(out, r_buf[k, j])
        return out

    def spread_rows(d):
        for t in range(TR_DEV):
            for blk in range(4):
                at = t * 4 + blk
                wide = jnp.broadcast_to(d[at : at + 1, :], (128, 128))
                by_row[t, blk * 128 : (blk + 1) * 128, :] = wide.T

    def z_refs(k, q):
        if k == 0:
            return z_buf0.at[q]
        return z_buf.at[k - 1, q]

    def z_from(k, p):
        return z_src0.at[p] if k == 0 else z_src.at[k - 1, p]

    def send_z(k):
        for q in range(NZ - 1, 0, -1):
            remote(
                z_from(k, Z_STEP[q] % 2), z_refs(k, q), z_send.at[k], z_recv.at[k, q], z_peer(q)
            ).start()

    def gather_z(k, targets, wait, total=False):
        join, _ = combine(total)

        def add(acc, value, at):
            acc = list(acc)
            for turn in range(4):
                v = pltpu.roll(value, 2 * turn, 0) if turn else value
                m = pltpu.roll(at, 2 * turn, 0) if turn else at
                for j in range(8):
                    acc[j] = join(acc[j], jnp.where(m == targets[j], v, 0.0))
            return tuple(acc)

        def body(q, acc):
            if wait:
                ref = z_refs(k, q)
                remote(ref, ref, z_send.at[k], z_recv.at[k, q], z_peer(1)).wait_recv()
            value = z_buf0[q, 0:8, :] if k == 0 else z_buf[k - 1, q]
            if k == 0 and wait:
                line = jnp.where(lane == iota, z_buf0[q, 8:9, :], -1.0)
                at = jnp.broadcast_to(jnp.max(line, axis=1, keepdims=True), (8, 128))
                meta_z[q] = at
            else:
                at = meta_z[q]
            return add(acc, value, at)

        own = z_src0[0, 0:8, :] if k == 0 else z_src[k - 1, 0]
        acc = add((jnp.zeros((8, 128), jnp.float32),) * 8, own, meta_src[...])
        return lax.fori_loop(1, NZ, body, acc)

    def send_slots(k):
        own = []
        for j in range(1, 8):
            dy, p = Y_STEP[j]
            at = meta_y[Y_STEP.index(((NY - dy) % NY, p))]
            own.append(jnp.where(at < 0, -2.0, at))
        first = jnp.where(meta_src[...] < 0, -2.0, meta_src[...])
        acc = gather_z(k, [first] + own, True)
        for j in range(8):
            y_src[k, j] = acc[j]
        for j in range(7, 0, -1):
            remote(
                y_src.at[k, j], y_buf.at[k, j % 2, j // 2], y_send.at[k], y_recv.at[k, j % 2],
                y_peer(j),
            ).start()

    def wait_slots(k, p):
        whole = y_buf.at[k, 1] if p else y_buf.at[k, 0, pl.ds(1, 3)]
        remote(whole, whole, y_send.at[k], y_recv.at[k, p], y_peer(1)).wait_recv()
        out = y_buf[k, 1, 0] if p else y_src[k, 0]
        for n in range(1, 4):
            out = jnp.maximum(out, y_buf[k, p, n])
        return out

    def next_rows(k, before, k_row, total=False):
        after = []
        for p in range(2):
            e = scaled(before[p], wait_slots(k, p))
            by_col[p] = e
            row_pass(k_row, p, total)
            after.append(e)
        send_rows(k_row)
        return after

    def dense(k, wait=False, total=False):
        every = [(4 * j + iota // 2).astype(jnp.float32) for j in range(8)]
        return gather_z(k, every, wait, total)

    def send_dense(k):
        for j, acc in enumerate(dense(k)):
            d_src[k, j] = acc
        for j in range(3, 0, -1):
            there = lax.rem(y + D_STEP[j], NY)
            remote(
                d_src.at[k, pl.ds(2 * there, 2)], d_buf.at[k, j], d_send.at[k], d_recv.at[k],
                d_peer(j),
            ).start()

    def send_totals():
        for j, acc in enumerate(dense(3, wait=True, total=True)):
            g_src[j] = acc
        for j in range(7, 0, -1):
            remote(g_src, g_buf.at[j], g_send, g_recv, y_peer(j)).start()

    def wait_dense(k):
        whole = d_buf.at[k, pl.ds(1, 3)]
        remote(whole, whole, d_send.at[k], d_recv.at[k], d_peer(1)).wait_recv()
        out = d_src[k, pl.ds(2 * y, 2)]
        for j in range(1, 4):
            out = jnp.maximum(out, d_buf[k, j])
        return out

    def columns_out():
        whole = f_buf.at[pl.ds(1, 7)]
        remote(whole, whole, f_send, f_recv, y_peer(1)).wait_recv()
        whole = g_buf.at[pl.ds(1, 7)]
        remote(whole, whole, g_send, g_recv, y_peer(1)).wait_recv()
        for g in range(4):
            dy = Y_STEP[2 * g][0]
            there = lax.rem(y - dy + NY, NY)
            for n in range(2):
                at = 2 * there + n
                sums = [g_src[at], g_buf[1, at]]
                for j in range(2, 8):
                    sums[j % 2] = sums[j % 2] + g_buf[j, at]
                near = scaled(f_src[n] if g == 0 else f_buf[2 * g, n], sums[0])
                far = scaled(f_buf[2 * g + 1, n], sums[1])
                low = jnp.where(half == 0, near, far)
                high = jnp.where(half == 0, far, near)
                for s in range(4):
                    at = (s % 2) * 4
                    col_out[there * 4 + n * 2 + s // 2, at : at + 2, :] = low[2 * s : 2 * s + 2, :]
                    col_out[there * 4 + n * 2 + s // 2, at + 2 : at + 4, :] = high[2 * s : 2 * s + 2, :]

    def wait_sends():
        for k in range(4):
            ref = z_buf0.at[pl.ds(1, 15)] if k == 0 else z_buf.at[k - 1, pl.ds(1, 15)]
            remote(ref, ref, z_send.at[k], z_recv.at[k, 1], z_peer(1)).wait_send()
            ref = r_buf.at[k, pl.ds(1, 7)]
            remote(ref, ref, r_send.at[k], r_recv.at[k], x_peer(1)).wait_send()
        for k in range(3):
            ref = d_buf.at[k, pl.ds(1, 3)]
            remote(ref, ref, d_send.at[k], d_recv.at[k], d_peer(1)).wait_send()
            ref = meta_y.at[pl.ds(1, 7)]
            remote(ref, ref, y_send.at[k], y_recv.at[k, 0], y_peer(1)).wait_send()
        ref = meta_y.at[pl.ds(1, 7)]
        remote(ref, ref, m_send, m_recv, y_peer(1)).wait_send()
        ref = f_buf.at[pl.ds(1, 7)]
        remote(ref, ref, f_send, f_recv, y_peer(1)).wait_send()
        ref = g_buf.at[pl.ds(1, 7)]
        remote(ref, ref, g_send, g_recv, y_peer(1)).wait_send()

    one = jnp.ones((8, 128), jnp.float32)
    first_pass()
    pl.semaphore_wait(barrier, len(peers))
    for q in (7, 8):
        pl.semaphore_signal(far_sem, inc=1, device_id=z_peer(q), device_id_type=MESH)
    send_rows(0)
    pl.semaphore_wait(far_sem, 2)
    send_z(0)
    for j in range(7, 0, -1):
        remote(meta_src, meta_y.at[j], m_send, m_recv, y_peer(j)).start()
    peak = wait_rows(0)
    d1 = scaled(one, peak)
    spread_rows(d1)
    column_pass(1)
    send_z(1)
    whole = meta_y.at[pl.ds(1, 7)]
    remote(whole, whole, m_send, m_recv, y_peer(1)).wait_recv()
    send_slots(0)
    send_dense(0)
    send_slots(1)
    e1 = next_rows(0, [one, one], 1)
    send_dense(1)
    e2 = next_rows(1, e1, 2)
    peak = wait_rows(1)
    d2 = scaled(d1, peak)
    spread_rows(d2)
    column_pass(2)
    send_z(2)
    peak = wait_rows(2)
    d3 = scaled(d2, peak)
    spread_rows(d3)
    column_pass(3, total=True)
    send_z(3)
    send_slots(2)
    send_dense(2)
    send_totals()
    mine = jnp.ones((2, 8, 128), jnp.float32)
    for k in range(3):
        mine = scaled(mine, wait_dense(k))
    f_src[...] = mine
    for j in range(7, 0, -1):
        remote(f_src, f_buf.at[j], f_send, f_recv, y_peer(j)).start()
    next_rows(2, e2, 3, total=True)
    columns_out()
    row_out[...] = scaled(d3, wait_rows(3, total=True))
    wait_sends()

def on_device(tiles, tile_list, tile_count):
    f32 = jnp.float32
    live = jnp.arange(SLOTS, dtype=jnp.int32)[None, :] < tile_count[:, None]
    facts = jnp.where(live, tile_list.T, -1)
    dma = pltpu.SemaphoreType.DMA
    row_scale, col_scale = pl.pallas_call(
        kernel,
        out_shape=(
            jax.ShapeDtypeStruct((8, 128), f32),
            jax.ShapeDtypeStruct((16, 8, 128), f32),
        ),
        in_specs=[
            pl.BlockSpec(memory_space=pltpu.VMEM),
            pl.BlockSpec(memory_space=pl.ANY),
        ],
        out_specs=(
            pl.BlockSpec(memory_space=pltpu.VMEM),
            pl.BlockSpec(memory_space=pltpu.VMEM),
        ),
        scratch_shapes=[
            pltpu.VMEM((SLOTS, TILE, TILE), f32),
            pltpu.VMEM((TR_DEV, TILE, 128), f32),
            pltpu.VMEM((2, 8, 128), f32),
            pltpu.VMEM((TR_DEV, TILE, 128), f32),
            pltpu.VMEM((2, 9, 128), f32),
            pltpu.VMEM((3, 2, 8, 128), f32),
            pltpu.VMEM((NZ, 9, 128), f32),
            pltpu.VMEM((3, NZ, 8, 128), f32),
            pltpu.VMEM((8, 128), f32),
            pltpu.VMEM((8, 8, 128), f32),
            pltpu.VMEM((NZ, 8, 128), f32),
            pltpu.VMEM((3, 8, 8, 128), f32),
            pltpu.VMEM((3, 2, 4, 8, 128), f32),
            pltpu.VMEM((3, 8, 8, 128), f32),
            pltpu.VMEM((3, 4, 2, 8, 128), f32),
            pltpu.VMEM((2, 8, 128), f32),
            pltpu.VMEM((8, 2, 8, 128), f32),
            pltpu.VMEM((8, 8, 128), f32),
            pltpu.VMEM((8, 8, 8, 128), f32),
            pltpu.VMEM((4, 8, 128), f32),
            pltpu.VMEM((4, 8, 8, 128), f32),
            dma((SLOTS,)),
            dma((4,)),
            dma((4, NZ)),
            dma,
            dma,
            dma((3,)),
            dma((3, 2)),
            dma((3,)),
            dma((3,)),
            dma,
            dma,
            dma,
            dma,
            dma((4,)),
            dma((4,)),
            pltpu.SemaphoreType.REGULAR,
        ],
        compiler_params=pltpu.CompilerParams(
            collective_id=0, has_side_effects=True, vmem_limit_bytes=52 * 1024 * 1024
        ),
    )(facts, tiles)
    return row_scale.reshape(-1), col_scale.reshape(-1)


def solution(mesh):
    return jax.shard_map(
        on_device,
        mesh=mesh,
        in_specs=(P(("row", "col"), None, None), P(("row", "col"), None), P(("row", "col"))),
        out_specs=(P("row"), P("col")),
        check_vma=False,
    )
```
